128 devices in a mesh: section: 8 (over z, y_lo), tensor: 16 (over y_hi, x, core).
Axes of the slice: x: 4, y: 4 (y_hi: 2, y_lo: 2; y = y_hi * 2 + y_lo), z: 4, core: 2. Of those that a mesh axis runs over, the one named last changes fastest.
Arguments:
- queries: bfloat16 [1024, 16384], P('section', 'tensor'), may hold values from -15 to 15
- tree_kv: bfloat16 [1024, 2, 1024], P('section'), may hold values from -6 to 6
- cache: bfloat16 [16, 8, 2, 8192, 128], P('section', None, None, 'tensor'), may hold values from -6 to 6
- cache_len: int32 [16], P('section'), may hold values from 1024 to 8192, as said below
- parents: int32 [16, 64], P('section'), may hold values from 0 to 62, as said below
- out_weight: bfloat16 [16384, 16384], P('tensor', 'section'), may hold values from -0.046875 to 0.046875
Outputs:
- projected: float32 [1024, 16384], P('tensor', 'section')
The draws below stay inside these ranges and needn't reach their ends.
Inputs may be any that keep to these rules, and one draw needn't show every extreme that they name: `cache_len`: some request holds a full cache of 8192 positions; every request holds at least 1024. parents[r, 0] = 0 for the root; for j >= 1, parents[r, j] < j.
All inputs are finite; a program needn't handle non-finite values.
Results may differ from the reference program's by a relative error of at most 0.0055.
Values may be sent and summed in bfloat16 or wider, within the bound.
A program may use at most 128 MiB of HBM per device.

```python
import math
import jax
import jax.numpy as jnp
from jax import lax

D = 16384
HEADS = 128
KVH = 8
HD = 128
TREE = 64
CACHE = 8192
REQS = 16
TOKENS = 1024


def draw_queries(key, part):
    values = 2.5 * jnp.clip(jax.random.normal(jax.random.fold_in(key, 1), (TOKENS, HEADS * HD), jnp.float32), -6.0, 6.0)
    return values.astype(jnp.bfloat16)


def draw_cache(key, part):
    values = jnp.clip(jax.random.normal(jax.random.fold_in(key, 2), (REQS, KVH, 2, CACHE, HD), jnp.float32), -6.0, 6.0)
    return values.astype(jnp.bfloat16)


def draw_cache_len(key, part):
    lengths = jax.random.randint(jax.random.fold_in(key, 3), (REQS,), CACHE // 8, CACHE + 1)
    chosen = jax.random.randint(jax.random.fold_in(key, 4), (), 0, REQS)
    return jnp.where(jnp.arange(REQS) == chosen, CACHE, lengths).astype(jnp.int32)


def draw_parents(key, part):
    columns = jnp.arange(TREE)
    upper = jnp.maximum(columns, 1)[None, :]
    drawn = jax.random.randint(jax.random.fold_in(key, 5), (REQS, TREE), 0, upper)
    chosen = jax.random.randint(jax.random.fold_in(key, 6), (), 0, REQS)
    last = (jnp.arange(REQS)[:, None] == chosen) & (columns[None, :] == TREE - 1)
    return jnp.where(last, TREE - 2, drawn).astype(jnp.int32)


def level_of(own_key, shape, shards, smallest, high):
    factor_of = 1.0
    for dim, blocks in shards:
        steps = jax.random.uniform(jax.random.fold_in(jax.random.fold_in(own_key, 6), dim), (blocks,), jnp.float32, smallest / len(shards), high / len(shards))
        factor_of = factor_of * jnp.repeat(jnp.exp(steps), shape[dim] // blocks).reshape((-1,) + (1,) * (len(shape) - 1 - dim))
    return factor_of


def bell_draw(stream_key, extent, deviation, most, shards=(), kind=jnp.bfloat16):
    factor_of = level_of(stream_key, extent, shards, -0.22, 0.18) if shards else 1.0
    array = jax.random.normal(stream_key, extent, jnp.float32) * deviation * factor_of
    return jnp.minimum(jnp.maximum(array, -most), most).astype(kind)


def setup_inputs(seed: int = 0) -> dict:
    arg_keys = jax.random.split(jax.random.key(seed), 7)
    queries = draw_queries(jax.random.fold_in(arg_keys[6], 71), 0)
    tree_kv = bell_draw(arg_keys[1], (TOKENS, 2, KVH * HD), 1.0, 6.0, ((0, 8),))
    cache = draw_cache(jax.random.fold_in(arg_keys[6], 71), 0)
    cache_len = draw_cache_len(jax.random.fold_in(arg_keys[6], 71), 0)
    parents = draw_parents(jax.random.fold_in(arg_keys[6], 71), 0)
    out_weight = bell_draw(arg_keys[5], (HEADS * HD, D), (HEADS * HD) ** -0.5, 0.046875, ((0, 16), (1, 8)))
    return dict(queries=queries, tree_kv=tree_kv, cache=cache, cache_len=cache_len, parents=parents, out_weight=out_weight)


NEGATIVE = -1e+30

def tree_reach(parent_rows):
    tree_size = parent_rows.shape[-1]
    places = jnp.arange(tree_size)
    linked = (places[None, None, :] == parent_rows[:, :, None]) & (places[None, :, None] >= 1)
    reached = (linked | (places[:, None] == places[None, :])[None]).astype(jnp.float32)
    for doubling in range(tree_size.bit_length()):
        reached = jnp.minimum(jnp.einsum('rij,rjk->rik', reached, reached, precision=lax.Precision.HIGHEST), 1.0)
    return reached > 0.5

def reference(queries, tree_kv, cache, cache_len, parents, out_weight):
    group = HEADS // KVH
    scale = 1.0 / math.sqrt(HD)
    reached = tree_reach(parents)
    positions = jnp.arange(CACHE)

    def one_request(items):
        block_queries, block_tree, block_cache, length, block_reach = items
        grouped = jnp.transpose(block_queries.reshape(TREE, KVH, group, HD), (1, 0, 2, 3)).astype(jnp.float32)
        tree_keys = jnp.transpose(block_tree[:, 0].reshape(TREE, KVH, HD), (1, 0, 2)).astype(jnp.float32)
        tree_values = jnp.transpose(block_tree[:, 1].reshape(TREE, KVH, HD), (1, 0, 2)).astype(jnp.float32)
        valid = positions < length

        def one_head(head_items):
            head_queries, head_cache, head_keys, head_values = head_items
            cache_keys = head_cache[0].astype(jnp.float32)
            cache_values = head_cache[1].astype(jnp.float32)
            cache_scores = jnp.einsum('tgd,pd->gtp', head_queries, cache_keys) * scale
            cache_scores = jnp.where(valid, cache_scores, NEGATIVE)
            own_scores = jnp.einsum('tgd,sd->gts', head_queries, head_keys) * scale
            own_scores = jnp.where(block_reach[None], own_scores, NEGATIVE)
            largest = jnp.maximum(lax.optimization_barrier(jnp.max(cache_scores, axis=-1)), lax.optimization_barrier(jnp.max(own_scores, axis=-1)))
            cache_weights = jnp.where(valid, jnp.exp(cache_scores - largest[..., None]), 0.0)
            own_weights = jnp.where(block_reach[None], jnp.exp(own_scores - largest[..., None]), 0.0)
            weight_total = lax.optimization_barrier(jnp.sum(cache_weights, axis=-1)) + lax.optimization_barrier(jnp.sum(own_weights, axis=-1))
            cache_rounded = lax.optimization_barrier(cache_weights.astype(jnp.bfloat16)).astype(jnp.float32)
            own_rounded = lax.optimization_barrier(own_weights.astype(jnp.bfloat16)).astype(jnp.float32)
            summed = jnp.einsum('gtp,pd->gtd', cache_rounded, cache_values)
            summed = summed + jnp.einsum('gts,sd->gtd', own_rounded, head_values)
            return summed / weight_total[..., None]
        heads_out = lax.map(one_head, (grouped, block_cache, tree_keys, tree_values))
        return jnp.transpose(heads_out, (2, 0, 1, 3)).reshape(TREE, HEADS * HD).astype(jnp.bfloat16)
    attended = lax.map(one_request, (queries.reshape(REQS, TREE, HEADS * HD), tree_kv.reshape(REQS, TREE, 2, KVH * HD), cache, cache_len, reached))
    attended = attended.reshape(TOKENS, HEADS * HD)
    return jnp.dot(attended, out_weight, preferred_element_type=jnp.float32)
```

```python
import functools
import math

import jax
import jax.numpy as jnp
from jax import lax
from jax.experimental import pallas as pl
from jax.experimental.pallas import tpu as pltpu
from jax.sharding import PartitionSpec as P

MESH = pl.DeviceIdType.MESH
F32 = jnp.float32
BF16 = jnp.bfloat16
MASKED = -1e30
LOWEST = -3000.0
LOG2E = 1.4426950408889634

RING = 4
SLOTS = 8
QK, PV, AT, PR = range(4)


def kernel(
    queries, tree_pair, cache, cache_len, parents, weight, out,
    q_buf, kv_buf, w_buf, tree_buf, bias, reach, o_buf, stats, tree_o, tree_stats,
    send_o, near_o, pair_o, full_o, a_buf, proj, send_p, near_p, pair_p, full_p, done_p, cross_p,
    local_sem, core_send, core_recv, send_sem, recv_sem,
):
    reqs, kv_heads = cache.shape[0], cache.shape[1]
    local_len, hd = cache.shape[3], cache.shape[4]
    half = q_buf.shape[3]
    tree_size = 2 * half
    wide = q_buf.shape[4]
    heads = wide // hd
    rows = heads * half
    groups = rows // 128
    cols = w_buf.shape[2]
    scale = LOG2E / math.sqrt(hd)

    section, tensor = lax.axis_index("section"), lax.axis_index("tensor")
    core = tensor % 2
    chip = tensor // 2
    x, yh = chip % 4, chip // 4
    z, yl = section // 2, section % 2

    def ring_t(d):
        return (section, yh * 8 + ((x + d) % 4) * 2 + core)

    def ring_s(d):
        return (((z + d) % 4) * 2 + yl, tensor)

    pair_t = (section, (1 - yh) * 8 + x * 2 + core)
    pair_s = (z * 2 + (1 - yl), tensor)
    other = (section, chip * 2 + (1 - core))

    def chip_of(slot):
        return ((yh + slot // 4) % 2) * 4 + (x + slot) % 4

    def section_of(slot):
        return ((z + slot) % 4) * 2 + (yl + slot // 4) % 2

    barrier = pltpu.get_barrier_semaphore()
    greeted = [ring_t(d) for d in (1, 2, 3)] + [ring_s(d) for d in (1, 2, 3)] + [pair_t, pair_s, other]
    for target in greeted:
        pl.semaphore_signal(barrier, inc=1, device_id=target, device_id_type=MESH)
    pl.semaphore_wait(barrier, len(greeted))

    def to_core(src, dst, number):
        return pltpu.make_async_remote_copy(
            src_ref=src, dst_ref=dst, send_sem=core_send.at[number], recv_sem=core_recv.at[number],
            device_id=other, device_id_type=MESH,
        )

    def remote(src, dst, phase, r, number, target):
        return pltpu.make_async_remote_copy(
            src_ref=src, dst_ref=dst, send_sem=send_sem.at[phase, r, number], recv_sem=recv_sem.at[phase, r, number],
            device_id=target, device_id_type=MESH,
        )

    def rows_of(r, which):
        return pl.ds(pl.multiple_of(r * tree_size + which * half, half), half)

    q_local = [
        pltpu.make_async_copy(queries.at[rows_of(r, core)], q_buf.at[r, 0, core], local_sem.at[r]) for r in range(reqs)
    ]
    q_cross = [to_core(queries.at[rows_of(r, 1 - core)], q_buf.at[r, 0, core], r) for r in range(reqs)]
    for r in range(reqs):
        q_cross[r].start()
        q_local[r].start()
    c_local = [pltpu.make_async_copy(cache.at[r], kv_buf.at[r, core], local_sem.at[2 + r]) for r in range(reqs)]
    c_cross = [to_core(cache.at[r], kv_buf.at[r, core], 2 + r) for r in range(reqs)]
    w_local = pltpu.make_async_copy(weight, w_buf.at[core], local_sem.at[4])
    w_cross = to_core(weight, w_buf.at[core], 4)
    t_local = pltpu.make_async_copy(tree_pair, tree_buf, local_sem.at[5])
    c_cross[0].start()
    c_local[0].start()
    t_local.start()

    def gather_first(buf, phase, r, ring, pair):
        copies = [remote(buf.at[r, 0], buf.at[r, 4], phase, r, 4, pair)]
        for d in (1, 3, 2):
            copies.append(remote(buf.at[r, 0], buf.at[r, 4 - d], phase, r, 4 - d, ring(d)))
        return copies

    def gather_ring(buf, phase, r, slot, pair):
        return remote(buf.at[r, slot, 1], buf.at[r, 4 + slot, 1], phase, r, 4 + slot, pair)

    def gather_pair(buf, phase, r, ring):
        return [remote(buf.at[r, 4, 0], buf.at[r, 8 - d, 0], phase, r, 11 - d, ring(d)) for d in (1, 3, 2)]

    def gather_arrived(buf, phase, r, slot, target):
        remote(buf.at[r, 0], buf.at[r, slot], phase, r, slot, target).wait_recv()

    def gather_halves_arrived(buf, phase, r, slot, target):
        remote(buf.at[r, 0, 1], buf.at[r, slot, 1], phase, r, slot, target).wait_recv()
        remote(buf.at[r, 0, 0], buf.at[r, slot, 0], phase, r, slot + 3, target).wait_recv()

    def start(copies):
        for copy in copies:
            copy.start()

    def scatter_near(src, near, pairs, phase, r, slot, ring, pair):
        d = slot - 4
        return [
            remote(src.at[r, slot, 1], pairs.at[r, d], phase, r, slot, pair),
            remote(src.at[r, slot, 0], near.at[r, 4 - d], phase, r, 11 - d, ring(d)),
        ]

    def scatter_near_arrived(src, near, pairs, phase, r, target):
        for d in (1, 2, 3):
            remote(src.at[r, 4 + d, 1], pairs.at[r, d], phase, r, 4 + d, target).wait_recv()
            remote(src.at[r, 4 + d, 0], near.at[r, d], phase, r, 7 + d, target).wait_recv()

    def scatter_full(src, full, phase, r, ring, pair):
        copies = [remote(src.at[r, 4], full.at[r, 4], phase, r, 4, pair)]
        for d in (1, 3, 2):
            copies.append(remote(src.at[r, d], full.at[r, 4 - d], phase, r, 4 - d, ring(d)))
        return copies

    def scatter_full_arrived(src, full, phase, r, target):
        for slot in (1, 2, 3, 4):
            remote(src.at[r, slot], full.at[r, slot], phase, r, slot, target).wait_recv()

    for r in range(reqs):
        q_local[r].wait()
        q_cross[r].wait_recv()
        if r == 0:
            start(gather_first(q_buf, QK, 0, ring_t, pair_t))
            c_cross[1].start()
            c_local[1].start()
            w_cross.start()
            w_local.start()

    sub8 = lax.broadcasted_iota(jnp.int32, (8, 128), 0)
    eye = lax.broadcasted_iota(jnp.int32, (128, 128), 0) == lax.broadcasted_iota(jnp.int32, (128, 128), 1)
    eye2 = jnp.concatenate([eye.astype(F32), eye.astype(F32)], axis=1) > 0.5
    ones2 = jnp.ones((256, 128), BF16)

    def column(row):
        high = row.astype(BF16).astype(F32)
        both = jnp.concatenate([high, row - high], axis=1)
        spread = jnp.where(eye2, jnp.broadcast_to(both, (128, 256)), 0.0).astype(BF16)
        return jnp.dot(spread, ones2, preferred_element_type=F32)

    def compact(tall):
        return jnp.sum(jnp.where(eye, tall, 0.0), axis=0, keepdims=True)

    def stat_block(peak, total):
        block = jnp.zeros((8, 128), F32)
        for g in range(groups):
            block = jnp.where(sub8 == g, compact(jnp.broadcast_to(peak[g * 128 : g * 128 + 128], (128, 128))), block)
            block = jnp.where(sub8 == groups + g, compact(total[g * 128 : g * 128 + 128]), block)
        return block

    jrow = lax.broadcasted_iota(jnp.int32, (128, 128), 0)
    icol = lax.broadcasted_iota(jnp.int32, (128, 128), 1)
    eye_small = lax.broadcasted_iota(jnp.int32, (tree_size, tree_size), 0) == lax.broadcasted_iota(
        jnp.int32, (tree_size, tree_size), 1
    )
    above = []
    for r in range(reqs):
        own = parents[r : r + 1, :].astype(F32)
        spread = jnp.where(eye_small, jnp.broadcast_to(own, (tree_size, tree_size)), 0.0).astype(BF16)
        above.append(jnp.dot(spread, jnp.ones((tree_size, 128), BF16), preferred_element_type=F32) + float(r * tree_size))
    above = jnp.concatenate(above, axis=0)
    linked = (icol.astype(F32) == above) & (jrow % tree_size >= 1)
    reached = jnp.where(linked | (jrow == icol), 1.0, 0.0)
    for _ in range((tree_size - 1).bit_length()):
        small = reached.astype(BF16)
        reached = jnp.minimum(jnp.dot(small, small, preferred_element_type=F32), 1.0)
    reach[...] = reached

    for r in range(reqs):
        place = lax.broadcasted_iota(jnp.int32, (2 * local_len, 128), 0) + chip * (2 * local_len)
        lane = lax.broadcasted_iota(jnp.int32, (2 * local_len, 128), 1)
        bias[r] = jnp.where((lane == 0) & (place >= cache_len[r]), MASKED, 0.0).astype(BF16)

    def stacked(block):
        return jnp.concatenate([block[:, h * hd : h * hd + hd] for h in range(heads)], axis=0)

    t_local.wait()

    def tree_step(step, _):
        r, a = step // 2, step % 2
        q = stacked(q_buf[r, 0, a])
        mask = jnp.concatenate([reach[rows_of(r, core), :]] * heads, axis=0) > 0.5
        s = lax.dot_general(q, tree_buf[0], (((1,), (1,)), ((), ())), preferred_element_type=F32) * scale
        s = jnp.where(mask, s, MASKED)
        peak = jnp.max(s, axis=1, keepdims=True).astype(BF16).astype(F32)
        w = jnp.where(mask, jnp.exp2(s - peak), 0.0).astype(BF16)
        v = jnp.concatenate([tree_buf[1], jnp.ones((128, 128), BF16)], axis=1)
        o = jnp.dot(w, v, preferred_element_type=F32)
        tree_o[r, a] = o[:, :hd]
        tree_stats[r, a] = stat_block(peak, o[:, hd:])
        return 0

    lax.fori_loop(0, 2 * reqs, tree_step, 0)

    def merge(parts):
        top = functools.reduce(jnp.maximum, [st for _, st in parts])
        factors = [jnp.exp2(st - top) for _, st in parts]
        totals = sum(st * pltpu.roll(f, groups, axis=0) for (_, st), f in zip(parts, factors))
        return top, factors, totals

    def merged_values(parts, factors):
        pieces = []
        for g in range(groups):
            piece = None
            for (value, _), f in zip(parts, factors):
                term = value[g * 128 : g * 128 + 128] * column(f[g : g + 1])
                piece = term if piece is None else piece + term
            pieces.append(piece)
        return pieces

    def put(ref, pieces, block):
        for g, piece in enumerate(pieces):
            ref[pl.ds(g * 128, 128), :] = piece.astype(BF16)
        high = block.astype(BF16).astype(F32)
        ref[pl.ds(rows, 16), :] = jnp.concatenate([high, block - high], axis=0).astype(BF16)

    def got(ref):
        tail = ref[pl.ds(rows, 16), :].astype(F32)
        return ref[pl.ds(0, rows), :].astype(F32), tail[:8] + tail[8:]

    def merge_into(ref, parts):
        top, factors, totals = merge(parts)
        block = jnp.where(sub8 < groups, top, jnp.where(sub8 < 2 * groups, totals, 0.0))
        put(ref, merged_values(parts, factors), block)

    def attend(r, slot):
        k = chip_of(slot)
        keys = jnp.concatenate([kv_buf[r, 0, k, 0], kv_buf[r, 1, k, 0]], axis=0)
        keys = jnp.concatenate([keys, bias[r]], axis=1)
        values = jnp.concatenate([kv_buf[r, 0, k, 1], kv_buf[r, 1, k, 1]], axis=0)
        values = jnp.concatenate([values, jnp.ones(values.shape, BF16)], axis=1)
        first = jnp.where(lax.broadcasted_iota(jnp.int32, (rows, 128), 1) == 0, 1.0, 0.0).astype(BF16)
        for a in range(2):
            q = jnp.concatenate([stacked(q_buf[r, slot, a]), first], axis=1)
            s = lax.dot_general(q, keys, (((1,), (1,)), ((), ())), preferred_element_type=F32)
            peak = jnp.maximum(jnp.max(s, axis=1, keepdims=True) * scale, LOWEST).astype(BF16).astype(F32)
            w = jnp.exp2(s * scale - peak).astype(BF16)
            o = jnp.dot(w, values, preferred_element_type=F32)
            o_buf[r, slot, a] = o[:, :hd]
            stats[r, slot, a] = stat_block(peak, o[:, hd:])

    def emit_own(r, slot, a):
        value = o_buf[r, slot, a]
        put(send_o.at[r, slot, a], [value[g * 128 : g * 128 + 128] for g in range(groups)], stats[r, slot, a])

    def scatter_sums(r):
        scatter_near_arrived(send_o, near_o, pair_o, PV, r, pair_t)
        merge_into(
            send_o.at[r, 4, 0],
            [(o_buf[r, 4, 0], stats[r, 4, 0])] + [got(near_o.at[r, d]) for d in (1, 2, 3)],
        )
        emit_own(r, 4, 1)
        copies = scatter_full(send_o, full_o, PV, r, ring_t, pair_t)
        copies[0].start()

        def ring_step(d, _):
            merge_into(send_o.at[r, d, 1], [(o_buf[r, d, 1], stats[r, d, 1]), got(pair_o.at[r, d])])
            emit_own(r, d, 0)
            return 0

        lax.fori_loop(1, RING, ring_step, 0)
        start(copies[1:])

    def finish_sums(r):
        scatter_full_arrived(send_o, full_o, PV, r, pair_t)

        def half_step(a, _):
            parts = [(o_buf[r, 0, a], stats[r, 0, a]), (tree_o[r, a], tree_stats[r, a])]
            parts += [got(full_o.at[r, slot, a]) for slot in (1, 2, 3, 4)]
            top, factors, totals = merge(parts)
            inverse = 1.0 / pltpu.roll(jnp.where((sub8 >= groups) & (sub8 < 2 * groups), totals, 1.0), 8 - groups, axis=0)
            factors = [f * inverse for f in factors]
            pieces = merged_values(parts, factors)
            per = 128 // half
            for h in range(heads):
                piece = pieces[h // per][(h % per) * half : (h % per + 1) * half]
                a_buf[r, 0, a, :, h * hd : h * hd + hd] = piece.astype(BF16)
            return 0

        lax.fori_loop(0, 2, half_step, 0)
        start(gather_first(a_buf, AT, r, ring_s, pair_s))

    def pass_attended(r):
        gather_arrived(a_buf, AT, r, 4, pair_s)
        start(gather_pair(a_buf, AT, r, ring_s))
        for d in (1, 3, 2):
            gather_arrived(a_buf, AT, r, d, pair_s)
            gather_ring(a_buf, AT, r, d, pair_s).start()

    def project(r):
        for slot in (5, 6, 7):
            gather_halves_arrived(a_buf, AT, r, slot, pair_s)
        step_cols = 512
        order = [section_of(slot) for slot in range(SLOTS)]

        def tile(n, _):
            at = pl.ds(pl.multiple_of(n * step_cols, step_cols), step_cols)
            acc = None
            for a in range(2):
                left = a_buf[r, :, a].reshape(SLOTS * half, wide)
                term = jnp.dot(left, w_buf[a, :, at], preferred_element_type=F32)
                acc = term if acc is None else acc + term
            for slot in range(SLOTS):
                proj[r, order[slot], :, at] = acc[slot * half : slot * half + half]
            return 0

        lax.fori_loop(0, cols // step_cols, tile, 0)

        for slot in (5, 6, 7):
            for a in range(2):
                send_p[r, slot, a] = proj[r, chip_of(slot), :, a * (cols // 2) : (a + 1) * (cols // 2)].astype(BF16)
            start(scatter_near(send_p, near_p, pair_p, PR, r, slot, ring_t, pair_t))

    def own_proj(r, slot, a):
        return proj[r, chip_of(slot), :, a * (cols // 2) : (a + 1) * (cols // 2)]

    def scatter_projected(r):
        scatter_near_arrived(send_p, near_p, pair_p, PR, r, pair_t)
        total = own_proj(r, 4, 0)
        for d in (1, 2, 3):
            total += near_p[r, d].astype(F32)
        send_p[r, 4, 0] = total.astype(BF16)
        send_p[r, 4, 1] = own_proj(r, 4, 1).astype(BF16)
        copies = scatter_full(send_p, full_p, PR, r, ring_t, pair_t)
        copies[0].start()
        for copy, d in zip(copies[1:], (1, 3, 2)):
            send_p[r, d, 0] = own_proj(r, d, 0).astype(BF16)
            send_p[r, d, 1] = (own_proj(r, d, 1) + pair_p[r, d].astype(F32)).astype(BF16)
            copy.start()

    def finish_projected(r):
        scatter_full_arrived(send_p, full_p, PR, r, pair_t)
        for a in range(2):
            total = own_proj(r, 0, a)
            for slot in (1, 2, 3, 4):
                total += full_p[r, slot, a].astype(F32)
            done_p[r, :, a * (cols // 2) : (a + 1) * (cols // 2)] = total

    def step(i, _):
        r, slot = i // SLOTS, i % SLOTS

        for number in range(reqs):

            @pl.when(i == number * SLOTS)
            def _():
                c_local[number].wait()
                c_cross[number].wait_recv()

        @pl.when(slot == 1)
        def _():
            gather_arrived(q_buf, QK, r, 4, pair_t)
            start(gather_pair(q_buf, QK, r, ring_t))

        @pl.when((slot >= 1) & (slot <= 3))
        def _():
            gather_arrived(q_buf, QK, r, slot, pair_t)
            gather_ring(q_buf, QK, r, slot, pair_t).start()

        @pl.when(i == 1)
        def _():
            start(gather_first(q_buf, QK, 1, ring_t, pair_t))

        @pl.when(slot >= 5)
        def _():
            gather_halves_arrived(q_buf, QK, r, slot, pair_t)

        @pl.when(i == SLOTS + 3)
        def _():
            scatter_sums(0)

        attend(r, slot)

        for last in (5, 6, 7):

            @pl.when(slot == last)
            def _():
                for a in range(2):
                    emit_own(r, last, a)
                start(scatter_near(send_o, near_o, pair_o, PV, r, last, ring_t, pair_t))

        return 0

    lax.fori_loop(0, reqs * SLOTS, step, 0)

    finish_sums(0)
    scatter_sums(1)
    pass_attended(0)
    finish_sums(1)
    w_local.wait()
    w_cross.wait_recv()
    project(0)
    pass_attended(1)
    scatter_projected(0)
    project(1)
    finish_projected(0)
    scatter_projected(1)
    finish_projected(1)

    crossing = to_core(done_p.at[1 - core], cross_p, 5)
    crossing.start()
    out[pl.ds(pl.multiple_of(core * half, half), half), :] = done_p[core]
    crossing.wait_recv()
    out[pl.ds(pl.multiple_of((1 - core) * half, half), half), :] = cross_p[...]

    for r in range(reqs):
        q_cross[r].wait_send()
        c_cross[r].wait_send()
    w_cross.wait_send()
    crossing.wait_send()
    for r in range(reqs):
        for phase, buf, ring, pair in ((QK, q_buf, ring_t, pair_t), (AT, a_buf, ring_s, pair_s)):
            copies = gather_first(buf, phase, r, ring, pair) + gather_pair(buf, phase, r, ring)
            copies += [gather_ring(buf, phase, r, d, pair) for d in (1, 2, 3)]
            for copy in copies:
                copy.wait_send()
        for phase, src, near, pairs, full in (
            (PV, send_o, near_o, pair_o, full_o),
            (PR, send_p, near_p, pair_p, full_p),
        ):
            copies = scatter_full(src, full, phase, r, ring_t, pair_t)
            for slot in (5, 6, 7):
                copies += scatter_near(src, near, pairs, phase, r, slot, ring_t, pair_t)
            for copy in copies:
                copy.wait_send()


def shards(queries, tree_kv, cache, cache_len, parents, out_weight):
    reqs, kv_heads, _, local_len, hd = cache.shape
    tokens, wide = queries.shape
    half = tokens // reqs // 2
    cols = out_weight.shape[1]
    rows = wide // hd * half
    kv = lax.axis_index("tensor") // 2
    tree_pair = jnp.swapaxes(lax.dynamic_slice_in_dim(tree_kv, kv * hd, hd, 2), 0, 1)
    hbm = pl.BlockSpec(memory_space=pl.ANY)
    vmem = pl.BlockSpec(memory_space=pltpu.VMEM)
    smem = pl.BlockSpec(memory_space=pltpu.SMEM)
    return pl.pallas_call(
        kernel,
        name="verify",
        out_shape=jax.ShapeDtypeStruct((2 * half, cols), F32),
        in_specs=[hbm, hbm, hbm, smem, vmem, hbm],
        out_specs=vmem,
        scratch_shapes=[
            pltpu.VMEM((reqs, SLOTS, 2, half, wide), BF16),
            pltpu.VMEM((reqs, 2, kv_heads, 2, local_len, hd), BF16),
            pltpu.VMEM((2, wide, cols), BF16),
            pltpu.VMEM((2, tokens, hd), BF16),
            pltpu.VMEM((reqs, 2 * local_len, 128), BF16),
            pltpu.VMEM((tokens, tokens), F32),
            pltpu.VMEM((reqs, SLOTS, 2, rows, hd), F32),
            pltpu.VMEM((reqs, SLOTS, 2, 8, 128), F32),
            pltpu.VMEM((reqs, 2, rows, hd), F32),
            pltpu.VMEM((reqs, 2, 8, 128), F32),
            pltpu.VMEM((reqs, SLOTS, 2, rows + 16, hd), BF16),
            pltpu.VMEM((reqs, RING, rows + 16, hd), BF16),
            pltpu.VMEM((reqs, RING, rows + 16, hd), BF16),
            pltpu.VMEM((reqs, 5, 2, rows + 16, hd), BF16),
            pltpu.VMEM((reqs, SLOTS, 2, half, wide), BF16),
            pltpu.VMEM((reqs, SLOTS, half, cols), F32),
            pltpu.VMEM((reqs, SLOTS, 2, half, cols // 2), BF16),
            pltpu.VMEM((reqs, RING, half, cols // 2), BF16),
            pltpu.VMEM((reqs, RING, half, cols // 2), BF16),
            pltpu.VMEM((reqs, 5, 2, half, cols // 2), BF16),
            pltpu.VMEM((reqs, half, cols), F32),
            pltpu.VMEM((half, cols), F32),
            pltpu.SemaphoreType.DMA((6,)),
            pltpu.SemaphoreType.DMA((6,)),
            pltpu.SemaphoreType.DMA((6,)),
            pltpu.SemaphoreType.DMA((4, reqs, 11)),
            pltpu.SemaphoreType.DMA((4, reqs, 11)),
        ],
        compiler_params=pltpu.CompilerParams(
            collective_id=0, has_side_effects=True, vmem_limit_bytes=60 * 2**20
        ),
        cost_estimate=pl.CostEstimate(flops=2 * 2**33, bytes_accessed=10 * 2**20, transcendentals=2**23),
    )(queries, tree_pair, cache, cache_len, parents, out_weight)


def solution(mesh):
    in_specs = (
        P("section", "tensor"),
        P("section", None, None),
        P("section", None, None, "tensor", None),
        P("section"),
        P("section", None),
        P("tensor", "section"),
    )
    out_specs = P("tensor", "section")
    return jax.shard_map(shards, mesh=mesh, in_specs=in_specs, out_specs=out_specs, check_vma=False)
```

```python
import functools
import math

import jax
import jax.numpy as jnp
from jax import lax
from jax.experimental import pallas as pl
from jax.experimental.pallas import tpu as pltpu
from jax.sharding import PartitionSpec as P

MESH = pl.DeviceIdType.MESH
F32 = jnp.float32
BF16 = jnp.bfloat16
MASKED = -1e30
LOWEST = -3000.0
LOG2E = 1.4426950408889634

RING = 4
SLOTS = 8
QK, PV, AT, PR = range(4)


def kernel(
    queries, tree_pair, cache, cache_len, parents, weight, out,
    q_buf, kv_buf, w_buf, tree_buf, bias, reach, o_buf, stats, tree_o, tree_stats,
    send_o, near_o, pair_o, full_o, a_buf, proj, send_p, near_p, pair_p, full_p, done_p, cross_p,
    local_sem, core_send, core_recv, send_sem, recv_sem,
):
    reqs, kv_heads = cache.shape[0], cache.shape[1]
    local_len, hd = cache.shape[3], cache.shape[4]
    half = q_buf.shape[3]
    tree_size = 2 * half
    wide = q_buf.shape[4]
    heads = wide // hd
    rows = heads * half
    groups = rows // 128
    cols = w_buf.shape[2]
    scale = LOG2E / math.sqrt(hd)

    section, tensor = lax.axis_index("section"), lax.axis_index("tensor")
    core = tensor % 2
    chip = tensor // 2
    x, yh = chip % 4, chip // 4
    z, yl = section // 2, section % 2

    def ring_t(d):
        return (section, yh * 8 + ((x + d) % 4) * 2 + core)

    def ring_s(d):
        return (((z + d) % 4) * 2 + yl, tensor)

    pair_t = (section, (1 - yh) * 8 + x * 2 + core)
    pair_s = (z * 2 + (1 - yl), tensor)
    other = (section, chip * 2 + (1 - core))

    def chip_of(slot):
        return ((yh + slot // 4) % 2) * 4 + (x + slot) % 4

    def section_of(slot):
        return ((z + slot) % 4) * 2 + (yl + slot // 4) % 2

    barrier = pltpu.get_barrier_semaphore()
    greeted = [ring_t(d) for d in (1, 2, 3)] + [ring_s(d) for d in (1, 2, 3)] + [pair_t, pair_s, other]
    for target in greeted:
        pl.semaphore_signal(barrier, inc=1, device_id=target, device_id_type=MESH)
    pl.semaphore_wait(barrier, len(greeted))

    def to_core(src, dst, number):
        return pltpu.make_async_remote_copy(
            src_ref=src, dst_ref=dst, send_sem=core_send.at[number], recv_sem=core_recv.at[number],
            device_id=other, device_id_type=MESH,
        )

    def remote(src, dst, phase, r, number, target):
        return pltpu.make_async_remote_copy(
            src_ref=src, dst_ref=dst, send_sem=send_sem.at[phase, r, number], recv_sem=recv_sem.at[phase, r, number],
            device_id=target, device_id_type=MESH,
        )

    def rows_of(r, which):
        return pl.ds(pl.multiple_of(r * tree_size + which * half, half), half)

    q_local = [
        pltpu.make_async_copy(queries.at[rows_of(r, core)], q_buf.at[r, 0, core], local_sem.at[r]) for r in range(reqs)
    ]
    q_cross = [to_core(queries.at[rows_of(r, 1 - core)], q_buf.at[r, 0, core], r) for r in range(reqs)]
    for r in range(reqs):
        q_cross[r].start()
        q_local[r].start()
    c_local = [pltpu.make_async_copy(cache.at[r], kv_buf.at[r, core], local_sem.at[2 + r]) for r in range(reqs)]
    c_cross = [to_core(cache.at[r], kv_buf.at[r, core], 2 + r) for r in range(reqs)]
    w_local = pltpu.make_async_copy(weight, w_buf.at[core], local_sem.at[4])
    w_cross = to_core(weight, w_buf.at[core], 4)
    t_local = pltpu.make_async_copy(tree_pair, tree_buf, local_sem.at[5])
    c_cross[0].start()
    c_local[0].start()
    t_local.start()

    def gather_first(buf, phase, r, ring, pair):
        copies = [remote(buf.at[r, 0], buf.at[r, 4], phase, r, 4, pair)]
        for d in (1, 3, 2):
            copies.append(remote(buf.at[r, 0], buf.at[r, 4 - d], phase, r, 4 - d, ring(d)))
        return copies

    def gather_ring(buf, phase, r, slot, pair):
        return remote(buf.at[r, slot, 1], buf.at[r, 4 + slot, 1], phase, r, 4 + slot, pair)

    def gather_pair(buf, phase, r, ring):
        return [remote(buf.at[r, 4, 0], buf.at[r, 8 - d, 0], phase, r, 11 - d, ring(d)) for d in (1, 3, 2)]

    def gather_arrived(buf, phase, r, slot, target):
        remote(buf.at[r, 0], buf.at[r, slot], phase, r, slot, target).wait_recv()

    def gather_halves_arrived(buf, phase, r, slot, target):
        remote(buf.at[r, 0, 1], buf.at[r, slot, 1], phase, r, slot, target).wait_recv()
        remote(buf.at[r, 0, 0], buf.at[r, slot, 0], phase, r, slot + 3, target).wait_recv()

    def start(copies):
        for copy in copies:
            copy.start()

    def scatter_near(src, near, pairs, phase, r, slot, ring, pair):
        d = slot - 4
        return [
            remote(src.at[r, slot, 1], pairs.at[r, d], phase, r, slot, pair),
            remote(src.at[r, slot, 0], near.at[r, 4 - d], phase, r, 11 - d, ring(d)),
        ]

    def scatter_near_arrived(src, near, pairs, phase, r, target):
        for d in (1, 2, 3):
            remote(src.at[r, 4 + d, 1], pairs.at[r, d], phase, r, 4 + d, target).wait_recv()
            remote(src.at[r, 4 + d, 0], near.at[r, d], phase, r, 7 + d, target).wait_recv()

    def scatter_full(src, full, phase, r, ring, pair):
        copies = [remote(src.at[r, 4], full.at[r, 4], phase, r, 4, pair)]
        for d in (1, 3, 2):
            copies.append(remote(src.at[r, d], full.at[r, 4 - d], phase, r, 4 - d, ring(d)))
        return copies

    def scatter_full_arrived(src, full, phase, r, target):
        for slot in (1, 2, 3, 4):
            remote(src.at[r, slot], full.at[r, slot], phase, r, slot, target).wait_recv()

    for r in range(reqs):
        q_local[r].wait()
        q_cross[r].wait_recv()
        if r == 0:
            start(gather_first(q_buf, QK, 0, ring_t, pair_t))
            c_cross[1].start()
            c_local[1].start()
            w_cross.start()
            w_local.start()

    sub8 = lax.broadcasted_iota(jnp.int32, (8, 128), 0)
    eye = lax.broadcasted_iota(jnp.int32, (128, 128), 0) == lax.broadcasted_iota(jnp.int32, (128, 128), 1)
    eye2 = jnp.concatenate([eye.astype(F32), eye.astype(F32)], axis=1) > 0.5
    ones2 = jnp.ones((256, 128), BF16)

    def column(row):
        high = row.astype(BF16).astype(F32)
        both = jnp.concatenate([high, row - high], axis=1)
        spread = jnp.where(eye2, jnp.broadcast_to(both, (128, 256)), 0.0).astype(BF16)
        return jnp.dot(spread, ones2, preferred_element_type=F32)

    def compact(tall):
        return jnp.sum(jnp.where(eye, tall, 0.0), axis=0, keepdims=True)

    def stat_block(peak, total):
        block = jnp.zeros((8, 128), F32)
        for g in range(groups):
            block = jnp.where(sub8 == g, compact(jnp.broadcast_to(peak[g * 128 : g * 128 + 128], (128, 128))), block)
            block = jnp.where(sub8 == groups + g, compact(total[g * 128 : g * 128 + 128]), block)
        return block

    jrow = lax.broadcasted_iota(jnp.int32, (128, 128), 0)
    icol = lax.broadcasted_iota(jnp.int32, (128, 128), 1)
    eye_small = lax.broadcasted_iota(jnp.int32, (tree_size, tree_size), 0) == lax.broadcasted_iota(
        jnp.int32, (tree_size, tree_size), 1
    )
    above = []
    for r in range(reqs):
        own = parents[r : r + 1, :].astype(F32)
        spread = jnp.where(eye_small, jnp.broadcast_to(own, (tree_size, tree_size)), 0.0).astype(BF16)
        above.append(jnp.dot(spread, jnp.ones((tree_size, 128), BF16), preferred_element_type=F32) + float(r * tree_size))
    above = jnp.concatenate(above, axis=0)
    linked = (icol.astype(F32) == above) & (jrow % tree_size >= 1)
    reached = jnp.where(linked | (jrow == icol), 1.0, 0.0)
    for _ in range((tree_size - 1).bit_length()):
        small = reached.astype(BF16)
        reached = jnp.minimum(jnp.dot(small, small, preferred_element_type=F32), 1.0)
    reach[...] = reached

    for r in range(reqs):
        place = lax.broadcasted_iota(jnp.int32, (2 * local_len, 128), 0) + chip * (2 * local_len)
        lane = lax.broadcasted_iota(jnp.int32, (2 * local_len, 128), 1)
        bias[r] = jnp.where((lane == 0) & (place >= cache_len[r]), MASKED, 0.0).astype(BF16)

    def stacked(block):
        return jnp.concatenate([block[:, h * hd : h * hd + hd] for h in range(heads)], axis=0)

    t_local.wait()

    def tree_step(step, _):
        r, a = step // 2, step % 2
        q = stacked(q_buf[r, 0, a])
        mask = jnp.concatenate([reach[rows_of(r, core), :]] * heads, axis=0) > 0.5
        s = lax.dot_general(q, tree_buf[0], (((1,), (1,)), ((), ())), preferred_element_type=F32) * scale
        s = jnp.where(mask, s, MASKED)
        peak = jnp.max(s, axis=1, keepdims=True).astype(BF16).astype(F32)
        w = jnp.where(mask, jnp.exp2(s - peak), 0.0).astype(BF16)
        v = jnp.concatenate([tree_buf[1], jnp.ones((128, 128), BF16)], axis=1)
        o = jnp.dot(w, v, preferred_element_type=F32)
        tree_o[r, a] = o[:, :hd]
        tree_stats[r, a] = stat_block(peak, o[:, hd:])
        return 0

    lax.fori_loop(0, 2 * reqs, tree_step, 0)

    def merge(parts):
        top = functools.reduce(jnp.maximum, [st for _, st in parts])
        factors = [jnp.exp2(st - top) for _, st in parts]
        totals = sum(st * pltpu.roll(f, groups, axis=0) for (_, st), f in zip(parts, factors))
        return top, factors, totals

    def merged_values(parts, factors):
        pieces = []
        for g in range(groups):
            piece = None
            for (value, _), f in zip(parts, factors):
                term = value[g * 128 : g * 128 + 128] * column(f[g : g + 1])
                piece = term if piece is None else piece + term
            pieces.append(piece)
        return pieces

    def put(ref, pieces, block):
        for g, piece in enumerate(pieces):
            ref[pl.ds(g * 128, 128), :] = piece.astype(BF16)
        high = block.astype(BF16).astype(F32)
        ref[pl.ds(rows, 16), :] = jnp.concatenate([high, block - high], axis=0).astype(BF16)

    def got(ref):
        tail = ref[pl.ds(rows, 16), :].astype(F32)
        return ref[pl.ds(0, rows), :].astype(F32), tail[:8] + tail[8:]

    def merge_into(ref, parts):
        top, factors, totals = merge(parts)
        block = jnp.where(sub8 < groups, top, jnp.where(sub8 < 2 * groups, totals, 0.0))
        put(ref, merged_values(parts, factors), block)

    def attend(r, slot):
        k = chip_of(slot)
        keys = jnp.concatenate([kv_buf[r, 0, k, 0], kv_buf[r, 1, k, 0]], axis=0)
        keys = jnp.concatenate([keys, bias[r]], axis=1)
        values = jnp.concatenate([kv_buf[r, 0, k, 1], kv_buf[r, 1, k, 1]], axis=0)
        values = jnp.concatenate([values, jnp.ones(values.shape, BF16)], axis=1)
        first = jnp.where(lax.broadcasted_iota(jnp.int32, (rows, 128), 1) == 0, 1.0, 0.0).astype(BF16)
        for a in range(2):
            q = jnp.concatenate([stacked(q_buf[r, slot, a]), first], axis=1)
            s = lax.dot_general(q, keys, (((1,), (1,)), ((), ())), preferred_element_type=F32)
            peak = jnp.maximum(jnp.max(s, axis=1, keepdims=True) * scale, LOWEST).astype(BF16).astype(F32)
            w = jnp.exp2(s * scale - peak).astype(BF16)
            o = jnp.dot(w, values, preferred_element_type=F32)
            o_buf[r, slot, a] = o[:, :hd]
            stats[r, slot, a] = stat_block(peak, o[:, hd:])

    def emit_own(r, slot, a):
        value = o_buf[r, slot, a]
        put(send_o.at[r, slot, a], [value[g * 128 : g * 128 + 128] for g in range(groups)], stats[r, slot, a])

    def scatter_sums(r):
        scatter_near_arrived(send_o, near_o, pair_o, PV, r, pair_t)
        merge_into(
            send_o.at[r, 4, 0],
            [(o_buf[r, 4, 0], stats[r, 4, 0])] + [got(near_o.at[r, d]) for d in (1, 2, 3)],
        )
        emit_own(r, 4, 1)
        copies = scatter_full(send_o, full_o, PV, r, ring_t, pair_t)
        copies[0].start()

        def ring_step(d, _):
            merge_into(send_o.at[r, d, 1], [(o_buf[r, d, 1], stats[r, d, 1]), got(pair_o.at[r, d])])
            emit_own(r, d, 0)
            return 0

        lax.fori_loop(1, RING, ring_step, 0)
        start(copies[1:])

    def finish_sums(r):
        scatter_full_arrived(send_o, full_o, PV, r, pair_t)

        def half_step(a, _):
            parts = [(o_buf[r, 0, a], stats[r, 0, a]), (tree_o[r, a], tree_stats[r, a])]
            parts += [got(full_o.at[r, slot, a]) for slot in (1, 2, 3, 4)]
            top, factors, totals = merge(parts)
            inverse = 1.0 / pltpu.roll(jnp.where((sub8 >= groups) & (sub8 < 2 * groups), totals, 1.0), 8 - groups, axis=0)
            factors = [f * inverse for f in factors]
            pieces = merged_values(parts, factors)
            per = 128 // half
            for h in range(heads):
                piece = pieces[h // per][(h % per) * half : (h % per + 1) * half]
                a_buf[r, 0, a, :, h * hd : h * hd + hd] = piece.astype(BF16)
            return 0

        lax.fori_loop(0, 2, half_step, 0)
        start(gather_first(a_buf, AT, r, ring_s, pair_s))

    def pass_whole(r):
        return [remote(a_buf.at[r, 4], a_buf.at[r, 8 - d], AT, r, 8 - d, ring_s(d)) for d in (1, 3, 2)]

    def pass_attended(r):
        gather_arrived(a_buf, AT, r, 4, pair_s)
        start(pass_whole(r))

    def project(r):
        for slot in (1, 2, 3, 5, 6, 7):
            gather_arrived(a_buf, AT, r, slot, pair_s)
        step_cols = 512
        order = [section_of(slot) for slot in range(SLOTS)]

        def tile(n, _):
            at = pl.ds(pl.multiple_of(n * step_cols, step_cols), step_cols)
            acc = None
            for a in range(2):
                left = a_buf[r, :, a].reshape(SLOTS * half, wide)
                term = jnp.dot(left, w_buf[a, :, at], preferred_element_type=F32)
                acc = term if acc is None else acc + term
            for slot in range(SLOTS):
                proj[r, order[slot], :, at] = acc[slot * half : slot * half + half]
            return 0

        lax.fori_loop(0, cols // step_cols, tile, 0)

        for slot in (5, 6, 7):
            for a in range(2):
                send_p[r, slot, a] = proj[r, chip_of(slot), :, a * (cols // 2) : (a + 1) * (cols // 2)].astype(BF16)
            start(scatter_near(send_p, near_p, pair_p, PR, r, slot, ring_t, pair_t))

    def own_proj(r, slot, a):
        return proj[r, chip_of(slot), :, a * (cols // 2) : (a + 1) * (cols // 2)]

    def scatter_projected(r):
        scatter_near_arrived(send_p, near_p, pair_p, PR, r, pair_t)
        total = own_proj(r, 4, 0)
        for d in (1, 2, 3):
            total += near_p[r, d].astype(F32)
        send_p[r, 4, 0] = total.astype(BF16)
        send_p[r, 4, 1] = own_proj(r, 4, 1).astype(BF16)
        copies = scatter_full(send_p, full_p, PR, r, ring_t, pair_t)
        copies[0].start()
        for copy, d in zip(copies[1:], (1, 3, 2)):
            send_p[r, d, 0] = own_proj(r, d, 0).astype(BF16)
            send_p[r, d, 1] = (own_proj(r, d, 1) + pair_p[r, d].astype(F32)).astype(BF16)
            copy.start()

    def finish_projected(r):
        scatter_full_arrived(send_p, full_p, PR, r, pair_t)
        for a in range(2):
            total = own_proj(r, 0, a)
            for slot in (1, 2, 3, 4):
                total += full_p[r, slot, a].astype(F32)
            done_p[r, :, a * (cols // 2) : (a + 1) * (cols // 2)] = total

    def step(i, _):
        r, slot = i // SLOTS, i % SLOTS

        for number in range(reqs):

            @pl.when(i == number * SLOTS)
            def _():
                c_local[number].wait()
                c_cross[number].wait_recv()

        @pl.when(slot == 1)
        def _():
            gather_arrived(q_buf, QK, r, 4, pair_t)
            start(gather_pair(q_buf, QK, r, ring_t))

        @pl.when((slot >= 1) & (slot <= 3))
        def _():
            gather_arrived(q_buf, QK, r, slot, pair_t)
            gather_ring(q_buf, QK, r, slot, pair_t).start()

        @pl.when(i == 1)
        def _():
            start(gather_first(q_buf, QK, 1, ring_t, pair_t))

        @pl.when(slot >= 5)
        def _():
            gather_halves_arrived(q_buf, QK, r, slot, pair_t)

        @pl.when(i == SLOTS + 3)
        def _():
            scatter_sums(0)

        attend(r, slot)

        for last in (5, 6, 7):

            @pl.when(slot == last)
            def _():
                for a in range(2):
                    emit_own(r, last, a)
                start(scatter_near(send_o, near_o, pair_o, PV, r, last, ring_t, pair_t))

        return 0

    lax.fori_loop(0, reqs * SLOTS, step, 0)

    finish_sums(0)
    scatter_sums(1)
    pass_attended(0)
    finish_sums(1)
    w_local.wait()
    w_cross.wait_recv()
    project(0)
    pass_attended(1)
    scatter_projected(0)
    project(1)
    finish_projected(0)
    scatter_projected(1)
    finish_projected(1)

    crossing = to_core(done_p.at[1 - core], cross_p, 5)
    crossing.start()
    out[pl.ds(pl.multiple_of(core * half, half), half), :] = done_p[core]
    crossing.wait_recv()
    out[pl.ds(pl.multiple_of((1 - core) * half, half), half), :] = cross_p[...]

    for r in range(reqs):
        q_cross[r].wait_send()
        c_cross[r].wait_send()
    w_cross.wait_send()
    crossing.wait_send()
    for r in range(reqs):
        copies = gather_first(q_buf, QK, r, ring_t, pair_t) + gather_pair(q_buf, QK, r, ring_t)
        copies += [gather_ring(q_buf, QK, r, d, pair_t) for d in (1, 2, 3)]
        copies += gather_first(a_buf, AT, r, ring_s, pair_s) + pass_whole(r)
        for copy in copies:
            copy.wait_send()
        for phase, src, near, pairs, full in (
            (PV, send_o, near_o, pair_o, full_o),
            (PR, send_p, near_p, pair_p, full_p),
        ):
            copies = scatter_full(src, full, phase, r, ring_t, pair_t)
            for slot in (5, 6, 7):
                copies += scatter_near(src, near, pairs, phase, r, slot, ring_t, pair_t)
            for copy in copies:
                copy.wait_send()


def shards(queries, tree_kv, cache, cache_len, parents, out_weight):
    reqs, kv_heads, _, local_len, hd = cache.shape
    tokens, wide = queries.shape
    half = tokens // reqs // 2
    cols = out_weight.shape[1]
    rows = wide // hd * half
    kv = lax.axis_index("tensor") // 2
    tree_pair = jnp.swapaxes(lax.dynamic_slice_in_dim(tree_kv, kv * hd, hd, 2), 0, 1)
    hbm = pl.BlockSpec(memory_space=pl.ANY)
    vmem = pl.BlockSpec(memory_space=pltpu.VMEM)
    smem = pl.BlockSpec(memory_space=pltpu.SMEM)
    return pl.pallas_call(
        kernel,
        name="verify",
        out_shape=jax.ShapeDtypeStruct((2 * half, cols), F32),
        in_specs=[hbm, hbm, hbm, smem, vmem, hbm],
        out_specs=vmem,
        scratch_shapes=[
            pltpu.VMEM((reqs, SLOTS, 2, half, wide), BF16),
            pltpu.VMEM((reqs, 2, kv_heads, 2, local_len, hd), BF16),
            pltpu.VMEM((2, wide, cols), BF16),
            pltpu.VMEM((2, tokens, hd), BF16),
            pltpu.VMEM((reqs, 2 * local_len, 128), BF16),
            pltpu.VMEM((tokens, tokens), F32),
            pltpu.VMEM((reqs, SLOTS, 2, rows, hd), F32),
            pltpu.VMEM((reqs, SLOTS, 2, 8, 128), F32),
            pltpu.VMEM((reqs, 2, rows, hd), F32),
            pltpu.VMEM((reqs, 2, 8, 128), F32),
            pltpu.VMEM((reqs, SLOTS, 2, rows + 16, hd), BF16),
            pltpu.VMEM((reqs, RING, rows + 16, hd), BF16),
            pltpu.VMEM((reqs, RING, rows + 16, hd), BF16),
            pltpu.VMEM((reqs, 5, 2, rows + 16, hd), BF16),
            pltpu.VMEM((reqs, SLOTS, 2, half, wide), BF16),
            pltpu.VMEM((reqs, SLOTS, half, cols), F32),
            pltpu.VMEM((reqs, SLOTS, 2, half, cols // 2), BF16),
            pltpu.VMEM((reqs, RING, half, cols // 2), BF16),
            pltpu.VMEM((reqs, RING, half, cols // 2), BF16),
            pltpu.VMEM((reqs, 5, 2, half, cols // 2), BF16),
            pltpu.VMEM((reqs, half, cols), F32),
            pltpu.VMEM((half, cols), F32),
            pltpu.SemaphoreType.DMA((6,)),
            pltpu.SemaphoreType.DMA((6,)),
            pltpu.SemaphoreType.DMA((6,)),
            pltpu.SemaphoreType.DMA((4, reqs, 11)),
            pltpu.SemaphoreType.DMA((4, reqs, 11)),
        ],
        compiler_params=pltpu.CompilerParams(
            collective_id=0, has_side_effects=True, vmem_limit_bytes=60 * 2**20
        ),
        cost_estimate=pl.CostEstimate(flops=2 * 2**33, bytes_accessed=10 * 2**20, transcendentals=2**23),
    )(queries, tree_pair, cache, cache_len, parents, out_weight)


def solution(mesh):
    in_specs = (
        P("section", "tensor"),
        P("section", None, None),
        P("section", None, None, "tensor", None),
        P("section"),
        P("section", None),
        P("tensor", "section"),
    )
    out_specs = P("tensor", "section")
    return jax.shard_map(shards, mesh=mesh, in_specs=in_specs, out_specs=out_specs, check_vma=False)
```

```python
import functools
import math

import jax
import jax.numpy as jnp
from jax import lax
from jax.experimental import pallas as pl
from jax.experimental.pallas import tpu as pltpu
from jax.sharding import PartitionSpec as P

MESH = pl.DeviceIdType.MESH
F32 = jnp.float32
BF16 = jnp.bfloat16
MASKED = -1e30
LOWEST = -3000.0
LOG2E = 1.4426950408889634

RING = 4
SLOTS = 8
QK, PV, AT, PR = range(4)


def kernel(
    queries, tree_pair, cache, cache_len, parents, weight, out,
    q_buf, kv_buf, w_buf, tree_buf, bias, reach, o_buf, stats, tree_o, tree_stats,
    send_o, near_o, pair_o, full_o, a_buf, proj, send_p, near_p, pair_p, full_p, done_p, cross_p,
    local_sem, core_send, core_recv, send_sem, recv_sem,
):
    reqs, kv_heads = cache.shape[0], cache.shape[1]
    local_len, hd = cache.shape[3], cache.shape[4]
    half = q_buf.shape[3]
    tree_size = 2 * half
    wide = q_buf.shape[4]
    heads = wide // hd
    rows = heads * half
    groups = rows // 128
    cols = w_buf.shape[2]
    scale = LOG2E / math.sqrt(hd)

    section, tensor = lax.axis_index("section"), lax.axis_index("tensor")
    core = tensor % 2
    chip = tensor // 2
    x, yh = chip % 4, chip // 4
    z, yl = section // 2, section % 2

    def ring_t(d):
        return (section, yh * 8 + ((x + d) % 4) * 2 + core)

    def ring_s(d):
        return (((z + d) % 4) * 2 + yl, tensor)

    pair_t = (section, (1 - yh) * 8 + x * 2 + core)
    pair_s = (z * 2 + (1 - yl), tensor)
    other = (section, chip * 2 + (1 - core))

    def chip_of(slot):
        return ((yh + slot // 4) % 2) * 4 + (x + slot) % 4

    def section_of(slot):
        return ((z + slot) % 4) * 2 + (yl + slot // 4) % 2

    barrier = pltpu.get_barrier_semaphore()
    greeted = [ring_t(d) for d in (1, 2, 3)] + [ring_s(d) for d in (1, 2, 3)] + [pair_t, pair_s, other]
    for target in greeted:
        pl.semaphore_signal(barrier, inc=1, device_id=target, device_id_type=MESH)
    pl.semaphore_wait(barrier, len(greeted))

    def to_core(src, dst, number):
        return pltpu.make_async_remote_copy(
            src_ref=src, dst_ref=dst, send_sem=core_send.at[number], recv_sem=core_recv.at[number],
            device_id=other, device_id_type=MESH,
        )

    def remote(src, dst, phase, r, number, target):
        return pltpu.make_async_remote_copy(
            src_ref=src, dst_ref=dst, send_sem=send_sem.at[phase, r, number], recv_sem=recv_sem.at[phase, r, number],
            device_id=target, device_id_type=MESH,
        )

    def rows_of(r, which):
        return pl.ds(pl.multiple_of(r * tree_size + which * half, half), half)

    q_local = [
        pltpu.make_async_copy(queries.at[rows_of(r, core)], q_buf.at[r, 0, core], local_sem.at[r]) for r in range(reqs)
    ]
    q_cross = [to_core(queries.at[rows_of(r, 1 - core)], q_buf.at[r, 0, core], r) for r in range(reqs)]
    for r in range(reqs):
        q_cross[r].start()
        q_local[r].start()
    c_local = [pltpu.make_async_copy(cache.at[r], kv_buf.at[r, core], local_sem.at[2 + r]) for r in range(reqs)]
    c_cross = [to_core(cache.at[r], kv_buf.at[r, core], 2 + r) for r in range(reqs)]
    w_local = pltpu.make_async_copy(weight, w_buf.at[core], local_sem.at[4])
    w_cross = to_core(weight, w_buf.at[core], 4)
    t_local = pltpu.make_async_copy(tree_pair, tree_buf, local_sem.at[5])
    c_cross[0].start()
    c_local[0].start()
    t_local.start()

    def gather_first(buf, phase, r, ring, pair):
        copies = [remote(buf.at[r, 0], buf.at[r, 4], phase, r, 4, pair)]
        for d in (1, 3, 2):
            copies.append(remote(buf.at[r, 0], buf.at[r, 4 - d], phase, r, 4 - d, ring(d)))
        return copies

    def gather_ring(buf, phase, r, slot, pair):
        return remote(buf.at[r, slot, 1], buf.at[r, 4 + slot, 1], phase, r, 4 + slot, pair)

    def gather_pair(buf, phase, r, ring):
        return [remote(buf.at[r, 4, 0], buf.at[r, 8 - d, 0], phase, r, 11 - d, ring(d)) for d in (1, 3, 2)]

    def gather_arrived(buf, phase, r, slot, target):
        remote(buf.at[r, 0], buf.at[r, slot], phase, r, slot, target).wait_recv()

    def gather_halves_arrived(buf, phase, r, slot, target):
        remote(buf.at[r, 0, 1], buf.at[r, slot, 1], phase, r, slot, target).wait_recv()
        remote(buf.at[r, 0, 0], buf.at[r, slot, 0], phase, r, slot + 3, target).wait_recv()

    def start(copies):
        for copy in copies:
            copy.start()

    def scatter_near(src, near, pairs, phase, r, slot, ring, pair):
        d = slot - 4
        return [
            remote(src.at[r, slot, 1], pairs.at[r, d], phase, r, slot, pair),
            remote(src.at[r, slot, 0], near.at[r, 4 - d], phase, r, 11 - d, ring(d)),
        ]

    def scatter_near_arrived(src, near, pairs, phase, r, target):
        for d in (1, 2, 3):
            remote(src.at[r, 4 + d, 1], pairs.at[r, d], phase, r, 4 + d, target).wait_recv()
            remote(src.at[r, 4 + d, 0], near.at[r, d], phase, r, 7 + d, target).wait_recv()

    def scatter_full(src, full, phase, r, ring, pair):
        copies = [remote(src.at[r, 4], full.at[r, 4], phase, r, 4, pair)]
        for d in (1, 3, 2):
            copies.append(remote(src.at[r, d], full.at[r, 4 - d], phase, r, 4 - d, ring(d)))
        return copies

    def scatter_full_arrived(src, full, phase, r, target):
        for slot in (1, 2, 3, 4):
            remote(src.at[r, slot], full.at[r, slot], phase, r, slot, target).wait_recv()

    for r in range(reqs):
        q_local[r].wait()
        q_cross[r].wait_recv()
        if r == 0:
            start(gather_first(q_buf, QK, 0, ring_t, pair_t))
            c_cross[1].start()
            c_local[1].start()
            w_cross.start()
            w_local.start()

    sub8 = lax.broadcasted_iota(jnp.int32, (8, 128), 0)
    eye = lax.broadcasted_iota(jnp.int32, (128, 128), 0) == lax.broadcasted_iota(jnp.int32, (128, 128), 1)
    eye2 = jnp.concatenate([eye.astype(F32), eye.astype(F32)], axis=1) > 0.5
    ones2 = jnp.ones((256, 128), BF16)

    def column(row):
        high = row.astype(BF16).astype(F32)
        both = jnp.concatenate([high, row - high], axis=1)
        spread = jnp.where(eye2, jnp.broadcast_to(both, (128, 256)), 0.0).astype(BF16)
        return jnp.dot(spread, ones2, preferred_element_type=F32)

    def compact(tall):
        return jnp.sum(jnp.where(eye, tall, 0.0), axis=0, keepdims=True)

    def stat_block(peak, total):
        block = jnp.zeros((8, 128), F32)
        for g in range(groups):
            block = jnp.where(sub8 == g, compact(jnp.broadcast_to(peak[g * 128 : g * 128 + 128], (128, 128))), block)
            block = jnp.where(sub8 == groups + g, compact(total[g * 128 : g * 128 + 128]), block)
        return block

    jrow = lax.broadcasted_iota(jnp.int32, (128, 128), 0)
    icol = lax.broadcasted_iota(jnp.int32, (128, 128), 1)
    eye_small = lax.broadcasted_iota(jnp.int32, (tree_size, tree_size), 0) == lax.broadcasted_iota(
        jnp.int32, (tree_size, tree_size), 1
    )
    above = []
    for r in range(reqs):
        own = parents[r : r + 1, :].astype(F32)
        spread = jnp.where(eye_small, jnp.broadcast_to(own, (tree_size, tree_size)), 0.0).astype(BF16)
        above.append(jnp.dot(spread, jnp.ones((tree_size, 128), BF16), preferred_element_type=F32) + float(r * tree_size))
    above = jnp.concatenate(above, axis=0)
    linked = (icol.astype(F32) == above) & (jrow % tree_size >= 1)
    reached = jnp.where(linked | (jrow == icol), 1.0, 0.0)
    for _ in range((tree_size - 1).bit_length()):
        small = reached.astype(BF16)
        reached = jnp.minimum(jnp.dot(small, small, preferred_element_type=F32), 1.0)
    reach[...] = reached

    for r in range(reqs):
        place = lax.broadcasted_iota(jnp.int32, (2 * local_len, 128), 0) + chip * (2 * local_len)
        lane = lax.broadcasted_iota(jnp.int32, (2 * local_len, 128), 1)
        bias[r] = jnp.where((lane == 0) & (place >= cache_len[r]), MASKED, 0.0).astype(BF16)

    def stacked(block):
        return jnp.concatenate([block[:, h * hd : h * hd + hd] for h in range(heads)], axis=0)

    t_local.wait()

    def tree_step(step, _):
        r, a = step // 2, step % 2
        q = stacked(q_buf[r, 0, a])
        mask = jnp.concatenate([reach[rows_of(r, core), :]] * heads, axis=0) > 0.5
        s = lax.dot_general(q, tree_buf[0], (((1,), (1,)), ((), ())), preferred_element_type=F32) * scale
        s = jnp.where(mask, s, MASKED)
        peak = jnp.max(s, axis=1, keepdims=True).astype(BF16).astype(F32)
        w = jnp.where(mask, jnp.exp2(s - peak), 0.0).astype(BF16)
        v = jnp.concatenate([tree_buf[1], jnp.ones((128, 128), BF16)], axis=1)
        o = jnp.dot(w, v, preferred_element_type=F32)
        tree_o[r, a] = o[:, :hd]
        tree_stats[r, a] = stat_block(peak, o[:, hd:])
        return 0

    lax.fori_loop(0, 2 * reqs, tree_step, 0)

    def merge(parts):
        top = functools.reduce(jnp.maximum, [st for _, st in parts])
        factors = [jnp.exp2(st - top) for _, st in parts]
        totals = sum(st * pltpu.roll(f, groups, axis=0) for (_, st), f in zip(parts, factors))
        return top, factors, totals

    def merged_values(parts, factors):
        pieces = []
        for g in range(groups):
            piece = None
            for (value, _), f in zip(parts, factors):
                term = value[g * 128 : g * 128 + 128] * column(f[g : g + 1])
                piece = term if piece is None else piece + term
            pieces.append(piece)
        return pieces

    def put(ref, pieces, block):
        for g, piece in enumerate(pieces):
            ref[pl.ds(g * 128, 128), :] = piece.astype(BF16)
        high = block.astype(BF16).astype(F32)
        ref[pl.ds(rows, 16), :] = jnp.concatenate([high, block - high], axis=0).astype(BF16)

    def got(ref):
        tail = ref[pl.ds(rows, 16), :].astype(F32)
        return ref[pl.ds(0, rows), :].astype(F32), tail[:8] + tail[8:]

    def merge_into(ref, parts):
        top, factors, totals = merge(parts)
        block = jnp.where(sub8 < groups, top, jnp.where(sub8 < 2 * groups, totals, 0.0))
        put(ref, merged_values(parts, factors), block)

    def attend(r, slot):
        k = chip_of(slot)
        keys = jnp.concatenate([kv_buf[r, 0, k, 0], kv_buf[r, 1, k, 0]], axis=0)
        keys = jnp.concatenate([keys, bias[r]], axis=1)
        values = jnp.concatenate([kv_buf[r, 0, k, 1], kv_buf[r, 1, k, 1]], axis=0)
        values = jnp.concatenate([values, jnp.ones(values.shape, BF16)], axis=1)
        first = jnp.where(lax.broadcasted_iota(jnp.int32, (rows, 128), 1) == 0, 1.0, 0.0).astype(BF16)
        for a in range(2):
            q = jnp.concatenate([stacked(q_buf[r, slot, a]), first], axis=1)
            s = lax.dot_general(q, keys, (((1,), (1,)), ((), ())), preferred_element_type=F32)
            peak = jnp.maximum(jnp.max(s, axis=1, keepdims=True) * scale, LOWEST).astype(BF16).astype(F32)
            w = jnp.exp2(s * scale - peak).astype(BF16)
            o = jnp.dot(w, values, preferred_element_type=F32)
            o_buf[r, slot, a] = o[:, :hd]
            stats[r, slot, a] = stat_block(peak, o[:, hd:])

    def emit_own(r, slot, a):
        value = o_buf[r, slot, a]
        put(send_o.at[r, slot, a], [value[g * 128 : g * 128 + 128] for g in range(groups)], stats[r, slot, a])

    def scatter_sums(r):
        scatter_near_arrived(send_o, near_o, pair_o, PV, r, pair_t)
        merge_into(
            send_o.at[r, 4, 0],
            [(o_buf[r, 4, 0], stats[r, 4, 0])] + [got(near_o.at[r, d]) for d in (1, 2, 3)],
        )
        emit_own(r, 4, 1)
        copies = scatter_full(send_o, full_o, PV, r, ring_t, pair_t)
        copies[0].start()

        for copy, d in zip(copies[1:], (1, 3, 2)):
            merge_into(send_o.at[r, d, 1], [(o_buf[r, d, 1], stats[r, d, 1]), got(pair_o.at[r, d])])
            emit_own(r, d, 0)
            copy.start()

    def finish_sums(r):
        scatter_full_arrived(send_o, full_o, PV, r, pair_t)

        def half_step(a, _):
            parts = [(o_buf[r, 0, a], stats[r, 0, a]), (tree_o[r, a], tree_stats[r, a])]
            parts += [got(full_o.at[r, slot, a]) for slot in (1, 2, 3, 4)]
            top, factors, totals = merge(parts)
            inverse = 1.0 / pltpu.roll(jnp.where((sub8 >= groups) & (sub8 < 2 * groups), totals, 1.0), 8 - groups, axis=0)
            factors = [f * inverse for f in factors]
            pieces = merged_values(parts, factors)
            per = 128 // half
            for h in range(heads):
                piece = pieces[h // per][(h % per) * half : (h % per + 1) * half]
                a_buf[r, 0, a, :, h * hd : h * hd + hd] = piece.astype(BF16)
            return 0

        lax.fori_loop(0, 2, half_step, 0)
        start(gather_first(a_buf, AT, r, ring_s, pair_s))

    def pass_whole(r):
        return [remote(a_buf.at[r, 4], a_buf.at[r, 8 - d], AT, r, 8 - d, ring_s(d)) for d in (1, 3, 2)]

    def pass_attended(r):
        gather_arrived(a_buf, AT, r, 4, pair_s)
        start(pass_whole(r))

    def project(r):
        for slot in (1, 2, 3, 5, 6, 7):
            gather_arrived(a_buf, AT, r, slot, pair_s)
        step_cols = 512
        order = [section_of(slot) for slot in range(SLOTS)]

        def tile(n, _):
            at = pl.ds(pl.multiple_of(n * step_cols, step_cols), step_cols)
            acc = None
            for a in range(2):
                left = a_buf[r, :, a].reshape(SLOTS * half, wide)
                term = jnp.dot(left, w_buf[a, :, at], preferred_element_type=F32)
                acc = term if acc is None else acc + term
            for slot in range(SLOTS):
                proj[r, order[slot], :, at] = acc[slot * half : slot * half + half]
            return 0

        steps = cols // step_cols // 2
        for a in (1, 0):
            lax.fori_loop(a * steps, (a + 1) * steps, tile, 0)
            for slot in (5, 7, 6):
                send_p[r, slot, a] = proj[r, chip_of(slot), :, a * (cols // 2) : (a + 1) * (cols // 2)].astype(BF16)
                scatter_near(send_p, near_p, pair_p, PR, r, slot, ring_t, pair_t)[1 - a].start()

    def own_proj(r, slot, a):
        return proj[r, chip_of(slot), :, a * (cols // 2) : (a + 1) * (cols // 2)]

    def scatter_projected(r):
        scatter_near_arrived(send_p, near_p, pair_p, PR, r, pair_t)
        total = own_proj(r, 4, 0)
        for d in (1, 2, 3):
            total += near_p[r, d].astype(F32)
        send_p[r, 4, 0] = total.astype(BF16)
        send_p[r, 4, 1] = own_proj(r, 4, 1).astype(BF16)
        copies = scatter_full(send_p, full_p, PR, r, ring_t, pair_t)
        copies[0].start()
        for copy, d in zip(copies[1:], (1, 3, 2)):
            send_p[r, d, 0] = own_proj(r, d, 0).astype(BF16)
            send_p[r, d, 1] = (own_proj(r, d, 1) + pair_p[r, d].astype(F32)).astype(BF16)
            copy.start()

    def finish_projected(r):
        scatter_full_arrived(send_p, full_p, PR, r, pair_t)
        for a in range(2):
            total = own_proj(r, 0, a)
            for slot in (1, 2, 3, 4):
                total += full_p[r, slot, a].astype(F32)
            done_p[r, :, a * (cols // 2) : (a + 1) * (cols // 2)] = total

    def step(i, _):
        r, slot = i // SLOTS, i % SLOTS

        for number in range(reqs):

            @pl.when(i == number * SLOTS)
            def _():
                c_local[number].wait()
                c_cross[number].wait_recv()

        @pl.when(slot == 1)
        def _():
            gather_arrived(q_buf, QK, r, 4, pair_t)
            start(gather_pair(q_buf, QK, r, ring_t))

        @pl.when((slot >= 1) & (slot <= 3))
        def _():
            gather_arrived(q_buf, QK, r, slot, pair_t)
            gather_ring(q_buf, QK, r, slot, pair_t).start()

        @pl.when(i == 1)
        def _():
            start(gather_first(q_buf, QK, 1, ring_t, pair_t))

        @pl.when(slot >= 5)
        def _():
            gather_halves_arrived(q_buf, QK, r, slot, pair_t)

        @pl.when(i == SLOTS + 2)
        def _():
            scatter_sums(0)

        attend(r, slot)

        for last in (5, 6, 7):

            @pl.when(slot == last)
            def _():
                for a in range(2):
                    emit_own(r, last, a)
                start(scatter_near(send_o, near_o, pair_o, PV, r, last, ring_t, pair_t))

        return 0

    lax.fori_loop(0, reqs * SLOTS, step, 0)

    finish_sums(0)
    scatter_sums(1)
    pass_attended(0)
    finish_sums(1)
    w_local.wait()
    w_cross.wait_recv()
    project(0)
    pass_attended(1)
    scatter_projected(0)
    project(1)
    finish_projected(0)
    scatter_projected(1)
    finish_projected(1)

    crossing = to_core(done_p.at[1 - core], cross_p, 5)
    crossing.start()
    out[pl.ds(pl.multiple_of(core * half, half), half), :] = done_p[core]
    crossing.wait_recv()
    out[pl.ds(pl.multiple_of((1 - core) * half, half), half), :] = cross_p[...]

    for r in range(reqs):
        q_cross[r].wait_send()
        c_cross[r].wait_send()
    w_cross.wait_send()
    crossing.wait_send()
    for r in range(reqs):
        copies = gather_first(q_buf, QK, r, ring_t, pair_t) + gather_pair(q_buf, QK, r, ring_t)
        copies += [gather_ring(q_buf, QK, r, d, pair_t) for d in (1, 2, 3)]
        copies += gather_first(a_buf, AT, r, ring_s, pair_s) + pass_whole(r)
        for copy in copies:
            copy.wait_send()
        for phase, src, near, pairs, full in (
            (PV, send_o, near_o, pair_o, full_o),
            (PR, send_p, near_p, pair_p, full_p),
        ):
            copies = scatter_full(src, full, phase, r, ring_t, pair_t)
            for slot in (5, 6, 7):
                copies += scatter_near(src, near, pairs, phase, r, slot, ring_t, pair_t)
            for copy in copies:
                copy.wait_send()


def shards(queries, tree_kv, cache, cache_len, parents, out_weight):
    reqs, kv_heads, _, local_len, hd = cache.shape
    tokens, wide = queries.shape
    half = tokens // reqs // 2
    cols = out_weight.shape[1]
    rows = wide // hd * half
    kv = lax.axis_index("tensor") // 2
    tree_pair = jnp.swapaxes(lax.dynamic_slice_in_dim(tree_kv, kv * hd, hd, 2), 0, 1)
    hbm = pl.BlockSpec(memory_space=pl.ANY)
    vmem = pl.BlockSpec(memory_space=pltpu.VMEM)
    smem = pl.BlockSpec(memory_space=pltpu.SMEM)
    return pl.pallas_call(
        kernel,
        name="verify",
        out_shape=jax.ShapeDtypeStruct((2 * half, cols), F32),
        in_specs=[hbm, hbm, hbm, smem, vmem, hbm],
        out_specs=vmem,
        scratch_shapes=[
            pltpu.VMEM((reqs, SLOTS, 2, half, wide), BF16),
            pltpu.VMEM((reqs, 2, kv_heads, 2, local_len, hd), BF16),
            pltpu.VMEM((2, wide, cols), BF16),
            pltpu.VMEM((2, tokens, hd), BF16),
            pltpu.VMEM((reqs, 2 * local_len, 128), BF16),
            pltpu.VMEM((tokens, tokens), F32),
            pltpu.VMEM((reqs, SLOTS, 2, rows, hd), F32),
            pltpu.VMEM((reqs, SLOTS, 2, 8, 128), F32),
            pltpu.VMEM((reqs, 2, rows, hd), F32),
            pltpu.VMEM((reqs, 2, 8, 128), F32),
            pltpu.VMEM((reqs, SLOTS, 2, rows + 16, hd), BF16),
            pltpu.VMEM((reqs, RING, rows + 16, hd), BF16),
            pltpu.VMEM((reqs, RING, rows + 16, hd), BF16),
            pltpu.VMEM((reqs, 5, 2, rows + 16, hd), BF16),
            pltpu.VMEM((reqs, SLOTS, 2, half, wide), BF16),
            pltpu.VMEM((reqs, SLOTS, half, cols), F32),
            pltpu.VMEM((reqs, SLOTS, 2, half, cols // 2), BF16),
            pltpu.VMEM((reqs, RING, half, cols // 2), BF16),
            pltpu.VMEM((reqs, RING, half, cols // 2), BF16),
            pltpu.VMEM((reqs, 5, 2, half, cols // 2), BF16),
            pltpu.VMEM((reqs, half, cols), F32),
            pltpu.VMEM((half, cols), F32),
            pltpu.SemaphoreType.DMA((6,)),
            pltpu.SemaphoreType.DMA((6,)),
            pltpu.SemaphoreType.DMA((6,)),
            pltpu.SemaphoreType.DMA((4, reqs, 11)),
            pltpu.SemaphoreType.DMA((4, reqs, 11)),
        ],
        compiler_params=pltpu.CompilerParams(
            collective_id=0, has_side_effects=True, vmem_limit_bytes=50 * 2**20
        ),
        cost_estimate=pl.CostEstimate(flops=2 * 2**33, bytes_accessed=10 * 2**20, transcendentals=2**23),
    )(queries, tree_pair, cache, cache_len, parents, out_weight)


def solution(mesh):
    in_specs = (
        P("section", "tensor"),
        P("section", None, None),
        P("section", None, None, "tensor", None),
        P("section"),
        P("section", None),
        P("tensor", "section"),
    )
    out_specs = P("tensor", "section")
    return jax.shard_map(shards, mesh=mesh, in_specs=in_specs, out_specs=out_specs, check_vma=False)
```

```python
import functools
import math

import jax
import jax.numpy as jnp
from jax import lax
from jax.experimental import pallas as pl
from jax.experimental.pallas import tpu as pltpu
from jax.sharding import PartitionSpec as P

MESH = pl.DeviceIdType.MESH
F32 = jnp.float32
BF16 = jnp.bfloat16
MASKED = -1e30
LOWEST = -3000.0
LOG2E = 1.4426950408889634

RING = 4
SLOTS = 8
QK, PV, AT, PR = range(4)


def kernel(
    queries, tree_pair, cache, cache_len, parents, weight, out,
    q_buf, kv_buf, w_buf, tree_buf, bias, reach, o_buf, stats, tree_o, tree_stats,
    send_o, near_o, pair_o, full_o, a_buf, proj, send_p, near_p, pair_p, full_p, done_p, cross_p,
    local_sem, core_send, core_recv, send_sem, recv_sem,
):
    reqs, kv_heads = cache.shape[0], cache.shape[1]
    local_len, hd = cache.shape[3], cache.shape[4]
    half = q_buf.shape[3]
    tree_size = 2 * half
    wide = q_buf.shape[4]
    heads = wide // hd
    rows = heads * half
    groups = rows // 128
    cols = w_buf.shape[2]
    scale = LOG2E / math.sqrt(hd)

    section, tensor = lax.axis_index("section"), lax.axis_index("tensor")
    core = tensor % 2
    chip = tensor // 2
    x, yh = chip % 4, chip // 4
    z, yl = section // 2, section % 2

    def ring_t(d):
        return (section, yh * 8 + ((x + d) % 4) * 2 + core)

    def ring_s(d):
        return (((z + d) % 4) * 2 + yl, tensor)

    pair_t = (section, (1 - yh) * 8 + x * 2 + core)
    pair_s = (z * 2 + (1 - yl), tensor)
    other = (section, chip * 2 + (1 - core))

    def chip_of(slot):
        return ((yh + slot // 4) % 2) * 4 + (x + slot) % 4

    def section_of(slot):
        return ((z + slot) % 4) * 2 + (yl + slot // 4) % 2

    barrier = pltpu.get_barrier_semaphore()
    greeted = [ring_t(d) for d in (1, 2, 3)] + [ring_s(d) for d in (1, 2, 3)] + [pair_t, pair_s, other]
    for target in greeted:
        pl.semaphore_signal(barrier, inc=1, device_id=target, device_id_type=MESH)

    def to_core(src, dst, number):
        return pltpu.make_async_remote_copy(
            src_ref=src, dst_ref=dst, send_sem=core_send.at[number], recv_sem=core_recv.at[number],
            device_id=other, device_id_type=MESH,
        )

    def remote(src, dst, phase, r, number, target):
        return pltpu.make_async_remote_copy(
            src_ref=src, dst_ref=dst, send_sem=send_sem.at[phase, r, number], recv_sem=recv_sem.at[phase, r, number],
            device_id=target, device_id_type=MESH,
        )

    def rows_of(r, which):
        return pl.ds(pl.multiple_of(r * tree_size + which * half, half), half)

    q_local = [
        pltpu.make_async_copy(queries.at[rows_of(r, core)], q_buf.at[r, 0, core], local_sem.at[r]) for r in range(reqs)
    ]
    q_cross = [to_core(queries.at[rows_of(r, 1 - core)], q_buf.at[r, 0, core], r) for r in range(reqs)]
    for r in range(reqs):
        q_local[r].start()
    pl.semaphore_wait(barrier, len(greeted))
    for r in range(reqs):
        q_cross[r].start()
    c_local = [pltpu.make_async_copy(cache.at[r], kv_buf.at[r, core], local_sem.at[2 + r]) for r in range(reqs)]
    c_cross = [to_core(cache.at[r], kv_buf.at[r, core], 2 + r) for r in range(reqs)]
    w_local = pltpu.make_async_copy(weight, w_buf.at[core], local_sem.at[4])
    w_cross = to_core(weight, w_buf.at[core], 4)
    t_local = pltpu.make_async_copy(tree_pair, tree_buf, local_sem.at[5])
    c_cross[0].start()
    c_local[0].start()
    t_local.start()

    def gather_first(buf, phase, r, ring, pair):
        copies = [remote(buf.at[r, 0], buf.at[r, 4], phase, r, 4, pair)]
        for d in (1, 3, 2):
            copies.append(remote(buf.at[r, 0], buf.at[r, 4 - d], phase, r, 4 - d, ring(d)))
        return copies

    def gather_ring(buf, phase, r, slot, pair):
        return remote(buf.at[r, slot, 1], buf.at[r, 4 + slot, 1], phase, r, 4 + slot, pair)

    def gather_pair(buf, phase, r, ring):
        return [remote(buf.at[r, 4, 0], buf.at[r, 8 - d, 0], phase, r, 11 - d, ring(d)) for d in (1, 3, 2)]

    def gather_arrived(buf, phase, r, slot, target):
        remote(buf.at[r, 0], buf.at[r, slot], phase, r, slot, target).wait_recv()

    def gather_halves_arrived(buf, phase, r, slot, target):
        remote(buf.at[r, 0, 1], buf.at[r, slot, 1], phase, r, slot, target).wait_recv()
        remote(buf.at[r, 0, 0], buf.at[r, slot, 0], phase, r, slot + 3, target).wait_recv()

    def start(copies):
        for copy in copies:
            copy.start()

    def scatter_near(src, near, pairs, phase, r, slot, ring, pair):
        d = slot - 4
        return [
            remote(src.at[r, slot, 1], pairs.at[r, d], phase, r, slot, pair),
            remote(src.at[r, slot, 0], near.at[r, 4 - d], phase, r, 11 - d, ring(d)),
        ]

    def scatter_near_arrived(src, near, pairs, phase, r, target):
        for d in (1, 2, 3):
            remote(src.at[r, 4 + d, 1], pairs.at[r, d], phase, r, 4 + d, target).wait_recv()
            remote(src.at[r, 4 + d, 0], near.at[r, d], phase, r, 7 + d, target).wait_recv()

    def scatter_full(src, full, phase, r, ring, pair):
        copies = [remote(src.at[r, 4], full.at[r, 4], phase, r, 4, pair)]
        for d in (1, 3, 2):
            copies.append(remote(src.at[r, d], full.at[r, 4 - d], phase, r, 4 - d, ring(d)))
        return copies

    def scatter_full_arrived(src, full, phase, r, target):
        for slot in (1, 2, 3, 4):
            remote(src.at[r, slot], full.at[r, slot], phase, r, slot, target).wait_recv()

    for r in range(reqs):
        q_local[r].wait()
        q_cross[r].wait_recv()
        if r == 0:
            start(gather_first(q_buf, QK, 0, ring_t, pair_t))
            c_cross[1].start()
            c_local[1].start()
            w_cross.start()
            w_local.start()

    sub8 = lax.broadcasted_iota(jnp.int32, (8, 128), 0)
    eye = lax.broadcasted_iota(jnp.int32, (128, 128), 0) == lax.broadcasted_iota(jnp.int32, (128, 128), 1)
    eye2 = jnp.concatenate([eye.astype(F32), eye.astype(F32)], axis=1) > 0.5
    ones2 = jnp.ones((256, 128), BF16)

    def column(row):
        high = row.astype(BF16).astype(F32)
        both = jnp.concatenate([high, row - high], axis=1)
        spread = jnp.where(eye2, jnp.broadcast_to(both, (128, 256)), 0.0).astype(BF16)
        return jnp.dot(spread, ones2, preferred_element_type=F32)

    def compact(tall):
        return jnp.sum(jnp.where(eye, tall, 0.0), axis=0, keepdims=True)

    def stat_block(peak, total):
        block = jnp.zeros((8, 128), F32)
        for g in range(groups):
            block = jnp.where(sub8 == g, compact(jnp.broadcast_to(peak[g * 128 : g * 128 + 128], (128, 128))), block)
            block = jnp.where(sub8 == groups + g, compact(total[g * 128 : g * 128 + 128]), block)
        return block

    jrow = lax.broadcasted_iota(jnp.int32, (128, 128), 0)
    icol = lax.broadcasted_iota(jnp.int32, (128, 128), 1)
    eye_small = lax.broadcasted_iota(jnp.int32, (tree_size, tree_size), 0) == lax.broadcasted_iota(
        jnp.int32, (tree_size, tree_size), 1
    )
    above = []
    for r in range(reqs):
        own = parents[r : r + 1, :].astype(F32)
        spread = jnp.where(eye_small, jnp.broadcast_to(own, (tree_size, tree_size)), 0.0).astype(BF16)
        above.append(jnp.dot(spread, jnp.ones((tree_size, 128), BF16), preferred_element_type=F32) + float(r * tree_size))
    above = jnp.concatenate(above, axis=0)
    linked = (icol.astype(F32) == above) & (jrow % tree_size >= 1)
    reached = jnp.where(linked | (jrow == icol), 1.0, 0.0)
    for _ in range((tree_size - 1).bit_length()):
        small = reached.astype(BF16)
        reached = jnp.minimum(jnp.dot(small, small, preferred_element_type=F32), 1.0)
    reach[...] = reached

    for r in range(reqs):
        place = lax.broadcasted_iota(jnp.int32, (2 * local_len, 128), 0) + chip * (2 * local_len)
        lane = lax.broadcasted_iota(jnp.int32, (2 * local_len, 128), 1)
        bias[r] = jnp.where((lane == 0) & (place >= cache_len[r]), MASKED, 0.0).astype(BF16)

    def stacked(block):
        return jnp.concatenate([block[:, h * hd : h * hd + hd] for h in range(heads)], axis=0)

    t_local.wait()

    def tree_step(step, _):
        r, a = step // 2, step % 2
        q = stacked(q_buf[r, 0, a])
        mask = jnp.concatenate([reach[rows_of(r, core), :]] * heads, axis=0) > 0.5
        s = lax.dot_general(q, tree_buf[0], (((1,), (1,)), ((), ())), preferred_element_type=F32) * scale
        s = jnp.where(mask, s, MASKED)
        peak = jnp.max(s, axis=1, keepdims=True).astype(BF16).astype(F32)
        w = jnp.where(mask, jnp.exp2(s - peak), 0.0).astype(BF16)
        v = jnp.concatenate([tree_buf[1], jnp.ones((128, 128), BF16)], axis=1)
        o = jnp.dot(w, v, preferred_element_type=F32)
        tree_o[r, a] = o[:, :hd]
        tree_stats[r, a] = stat_block(peak, o[:, hd:])
        return 0

    lax.fori_loop(0, 2 * reqs, tree_step, 0)

    def merge(parts):
        top = functools.reduce(jnp.maximum, [st for _, st in parts])
        factors = [jnp.exp2(st - top) for _, st in parts]
        totals = sum(st * pltpu.roll(f, groups, axis=0) for (_, st), f in zip(parts, factors))
        return top, factors, totals

    def merged_values(parts, factors):
        pieces = []
        for g in range(groups):
            piece = None
            for (value, _), f in zip(parts, factors):
                term = value[g * 128 : g * 128 + 128] * column(f[g : g + 1])
                piece = term if piece is None else piece + term
            pieces.append(piece)
        return pieces

    def put(ref, pieces, block):
        for g, piece in enumerate(pieces):
            ref[pl.ds(g * 128, 128), :] = piece.astype(BF16)
        high = block.astype(BF16).astype(F32)
        ref[pl.ds(rows, 16), :] = jnp.concatenate([high, block - high], axis=0).astype(BF16)

    def got(ref):
        tail = ref[pl.ds(rows, 16), :].astype(F32)
        return ref[pl.ds(0, rows), :].astype(F32), tail[:8] + tail[8:]

    def merge_into(ref, parts):
        top, factors, totals = merge(parts)
        block = jnp.where(sub8 < groups, top, jnp.where(sub8 < 2 * groups, totals, 0.0))
        put(ref, merged_values(parts, factors), block)

    def attend(r, slot):
        k = chip_of(slot)
        keys = jnp.concatenate([kv_buf[r, 0, k, 0], kv_buf[r, 1, k, 0]], axis=0)
        keys = jnp.concatenate([keys, bias[r]], axis=1)
        values = jnp.concatenate([kv_buf[r, 0, k, 1], kv_buf[r, 1, k, 1]], axis=0)
        values = jnp.concatenate([values, jnp.ones(values.shape, BF16)], axis=1)
        first = jnp.where(lax.broadcasted_iota(jnp.int32, (rows, 128), 1) == 0, 1.0, 0.0).astype(BF16)
        for a in range(2):
            q = jnp.concatenate([stacked(q_buf[r, slot, a]), first], axis=1)
            s = lax.dot_general(q, keys, (((1,), (1,)), ((), ())), preferred_element_type=F32)
            peak = jnp.maximum(jnp.max(s, axis=1, keepdims=True) * scale, LOWEST).astype(BF16).astype(F32)
            w = jnp.exp2(s * scale - peak).astype(BF16)
            o = jnp.dot(w, values, preferred_element_type=F32)
            o_buf[r, slot, a] = o[:, :hd]
            stats[r, slot, a] = stat_block(peak, o[:, hd:])

    def emit_own(r, slot, a):
        value = o_buf[r, slot, a]
        put(send_o.at[r, slot, a], [value[g * 128 : g * 128 + 128] for g in range(groups)], stats[r, slot, a])

    def scatter_sums(r):
        scatter_near_arrived(send_o, near_o, pair_o, PV, r, pair_t)
        merge_into(
            send_o.at[r, 4, 0],
            [(o_buf[r, 4, 0], stats[r, 4, 0])] + [got(near_o.at[r, d]) for d in (1, 2, 3)],
        )
        emit_own(r, 4, 1)
        copies = scatter_full(send_o, full_o, PV, r, ring_t, pair_t)
        copies[0].start()

        for copy, d in zip(copies[1:], (1, 3, 2)):
            merge_into(send_o.at[r, d, 1], [(o_buf[r, d, 1], stats[r, d, 1]), got(pair_o.at[r, d])])
            emit_own(r, d, 0)
            copy.start()

    def finish_sums(r):
        scatter_full_arrived(send_o, full_o, PV, r, pair_t)

        def half_step(a, _):
            parts = [(o_buf[r, 0, a], stats[r, 0, a]), (tree_o[r, a], tree_stats[r, a])]
            parts += [got(full_o.at[r, slot, a]) for slot in (1, 2, 3, 4)]
            top, factors, totals = merge(parts)
            inverse = 1.0 / pltpu.roll(jnp.where((sub8 >= groups) & (sub8 < 2 * groups), totals, 1.0), 8 - groups, axis=0)
            factors = [f * inverse for f in factors]
            pieces = merged_values(parts, factors)
            per = 128 // half
            for h in range(heads):
                piece = pieces[h // per][(h % per) * half : (h % per + 1) * half]
                a_buf[r, 0, a, :, h * hd : h * hd + hd] = piece.astype(BF16)
            return 0

        lax.fori_loop(0, 2, half_step, 0)
        start(gather_first(a_buf, AT, r, ring_s, pair_s))

    def pass_whole(r):
        return [remote(a_buf.at[r, 4], a_buf.at[r, 8 - d], AT, r, 8 - d, ring_s(d)) for d in (1, 3, 2)]

    def pass_attended(r):
        gather_arrived(a_buf, AT, r, 4, pair_s)
        start(pass_whole(r))

    def project(r):
        for slot in (1, 2, 3, 5, 6, 7):
            gather_arrived(a_buf, AT, r, slot, pair_s)
        step_cols = 512
        order = [section_of(slot) for slot in range(SLOTS)]

        def tile(n, _):
            at = pl.ds(pl.multiple_of(n * step_cols, step_cols), step_cols)
            acc = None
            for a in range(2):
                left = a_buf[r, :, a].reshape(SLOTS * half, wide)
                term = jnp.dot(left, w_buf[a, :, at], preferred_element_type=F32)
                acc = term if acc is None else acc + term
            for slot in range(SLOTS):
                proj[r, order[slot], :, at] = acc[slot * half : slot * half + half]
            return 0

        steps = cols // step_cols // 2
        for a in (1, 0):
            lax.fori_loop(a * steps, (a + 1) * steps, tile, 0)
            for slot in (5, 7, 6):
                send_p[r, slot, a] = proj[r, chip_of(slot), :, a * (cols // 2) : (a + 1) * (cols // 2)].astype(BF16)
                scatter_near(send_p, near_p, pair_p, PR, r, slot, ring_t, pair_t)[1 - a].start()

    def own_proj(r, slot, a):
        return proj[r, chip_of(slot), :, a * (cols // 2) : (a + 1) * (cols // 2)]

    def scatter_projected(r):
        scatter_near_arrived(send_p, near_p, pair_p, PR, r, pair_t)
        total = own_proj(r, 4, 0)
        for d in (1, 2, 3):
            total += near_p[r, d].astype(F32)
        send_p[r, 4, 0] = total.astype(BF16)
        send_p[r, 4, 1] = own_proj(r, 4, 1).astype(BF16)
        copies = scatter_full(send_p, full_p, PR, r, ring_t, pair_t)
        copies[0].start()
        for copy, d in zip(copies[1:], (1, 3, 2)):
            send_p[r, d, 0] = own_proj(r, d, 0).astype(BF16)
            send_p[r, d, 1] = (own_proj(r, d, 1) + pair_p[r, d].astype(F32)).astype(BF16)
            copy.start()

    def finish_projected(r):
        scatter_full_arrived(send_p, full_p, PR, r, pair_t)
        for a in range(2):
            total = own_proj(r, 0, a)
            for slot in (1, 2, 3, 4):
                total += full_p[r, slot, a].astype(F32)
            done_p[r, :, a * (cols // 2) : (a + 1) * (cols // 2)] = total

    def step(i, _):
        r, slot = i // SLOTS, i % SLOTS

        for number in range(reqs):

            @pl.when(i == number * SLOTS)
            def _():
                c_local[number].wait()
                c_cross[number].wait_recv()

        @pl.when(slot == 1)
        def _():
            gather_arrived(q_buf, QK, r, 4, pair_t)
            start(gather_pair(q_buf, QK, r, ring_t))

        @pl.when((slot >= 1) & (slot <= 3))
        def _():
            gather_arrived(q_buf, QK, r, slot, pair_t)
            gather_ring(q_buf, QK, r, slot, pair_t).start()

        @pl.when(i == 1)
        def _():
            start(gather_first(q_buf, QK, 1, ring_t, pair_t))

        @pl.when(slot >= 5)
        def _():
            gather_halves_arrived(q_buf, QK, r, slot, pair_t)

        @pl.when(i == SLOTS + 2)
        def _():
            scatter_sums(0)

        attend(r, slot)

        for last in (5, 6, 7):

            @pl.when(slot == last)
            def _():
                for a in range(2):
                    emit_own(r, last, a)
                start(scatter_near(send_o, near_o, pair_o, PV, r, last, ring_t, pair_t))

        return 0

    lax.fori_loop(0, reqs * SLOTS, step, 0)

    finish_sums(0)
    scatter_sums(1)
    pass_attended(0)
    finish_sums(1)
    w_local.wait()
    w_cross.wait_recv()
    project(0)
    pass_attended(1)
    scatter_projected(0)
    project(1)
    scatter_projected(1)
    finish_projected(0)
    finish_projected(1)

    crossing = to_core(done_p.at[1 - core], cross_p, 5)
    crossing.start()
    out[pl.ds(pl.multiple_of(core * half, half), half), :] = done_p[core]
    crossing.wait_recv()
    out[pl.ds(pl.multiple_of((1 - core) * half, half), half), :] = cross_p[...]

    for r in range(reqs):
        q_cross[r].wait_send()
        c_cross[r].wait_send()
    w_cross.wait_send()
    crossing.wait_send()
    for r in range(reqs):
        copies = gather_first(q_buf, QK, r, ring_t, pair_t) + gather_pair(q_buf, QK, r, ring_t)
        copies += [gather_ring(q_buf, QK, r, d, pair_t) for d in (1, 2, 3)]
        copies += gather_first(a_buf, AT, r, ring_s, pair_s) + pass_whole(r)
        for copy in copies:
            copy.wait_send()
        for phase, src, near, pairs, full in (
            (PV, send_o, near_o, pair_o, full_o),
            (PR, send_p, near_p, pair_p, full_p),
        ):
            copies = scatter_full(src, full, phase, r, ring_t, pair_t)
            for slot in (5, 6, 7):
                copies += scatter_near(src, near, pairs, phase, r, slot, ring_t, pair_t)
            for copy in copies:
                copy.wait_send()


def shards(queries, tree_kv, cache, cache_len, parents, out_weight):
    reqs, kv_heads, _, local_len, hd = cache.shape
    tokens, wide = queries.shape
    half = tokens // reqs // 2
    cols = out_weight.shape[1]
    rows = wide // hd * half
    kv = lax.axis_index("tensor") // 2
    tree_pair = jnp.swapaxes(lax.dynamic_slice_in_dim(tree_kv, kv * hd, hd, 2), 0, 1)
    hbm = pl.BlockSpec(memory_space=pl.ANY)
    vmem = pl.BlockSpec(memory_space=pltpu.VMEM)
    smem = pl.BlockSpec(memory_space=pltpu.SMEM)
    return pl.pallas_call(
        kernel,
        name="verify",
        out_shape=jax.ShapeDtypeStruct((2 * half, cols), F32),
        in_specs=[hbm, hbm, hbm, smem, vmem, hbm],
        out_specs=vmem,
        scratch_shapes=[
            pltpu.VMEM((reqs, SLOTS, 2, half, wide), BF16),
            pltpu.VMEM((reqs, 2, kv_heads, 2, local_len, hd), BF16),
            pltpu.VMEM((2, wide, cols), BF16),
            pltpu.VMEM((2, tokens, hd), BF16),
            pltpu.VMEM((reqs, 2 * local_len, 128), BF16),
            pltpu.VMEM((tokens, tokens), F32),
            pltpu.VMEM((reqs, SLOTS, 2, rows, hd), F32),
            pltpu.VMEM((reqs, SLOTS, 2, 8, 128), F32),
            pltpu.VMEM((reqs, 2, rows, hd), F32),
            pltpu.VMEM((reqs, 2, 8, 128), F32),
            pltpu.VMEM((reqs, SLOTS, 2, rows + 16, hd), BF16),
            pltpu.VMEM((reqs, RING, rows + 16, hd), BF16),
            pltpu.VMEM((reqs, RING, rows + 16, hd), BF16),
            pltpu.VMEM((reqs, 5, 2, rows + 16, hd), BF16),
            pltpu.VMEM((reqs, SLOTS, 2, half, wide), BF16),
            pltpu.VMEM((reqs, SLOTS, half, cols), F32),
            pltpu.VMEM((reqs, SLOTS, 2, half, cols // 2), BF16),
            pltpu.VMEM((reqs, RING, half, cols // 2), BF16),
            pltpu.VMEM((reqs, RING, half, cols // 2), BF16),
            pltpu.VMEM((reqs, 5, 2, half, cols // 2), BF16),
            pltpu.VMEM((reqs, half, cols), F32),
            pltpu.VMEM((half, cols), F32),
            pltpu.SemaphoreType.DMA((6,)),
            pltpu.SemaphoreType.DMA((6,)),
            pltpu.SemaphoreType.DMA((6,)),
            pltpu.SemaphoreType.DMA((4, reqs, 11)),
            pltpu.SemaphoreType.DMA((4, reqs, 11)),
        ],
        compiler_params=pltpu.CompilerParams(
            collective_id=0, has_side_effects=True, vmem_limit_bytes=50 * 2**20
        ),
        cost_estimate=pl.CostEstimate(flops=2 * 2**33, bytes_accessed=10 * 2**20, transcendentals=2**23),
    )(queries, tree_pair, cache, cache_len, parents, out_weight)


def solution(mesh):
    in_specs = (
        P("section", "tensor"),
        P("section", None, None),
        P("section", None, None, "tensor", None),
        P("section"),
        P("section", None),
        P("tensor", "section"),
    )
    out_specs = P("tensor", "section")
    return jax.shard_map(shards, mesh=mesh, in_specs=in_specs, out_specs=out_specs, check_vma=False)
```
